256 devices in a mesh: row: 64 (over x, z, core), col: 4 (over y).
Axes of the slice: x: 4, y: 4, z: 8, core: 2. Of those that a mesh axis runs over, the one named last changes fastest.
Arguments:
- margin: bfloat16 [24576, 24576], P('row', 'col'), may hold values from -0.109375 to 0.109375
- margin_pattern: int32 [96, 96], replicated, may hold values from 0 to 1, as said below
- orbitals_a: bfloat16 [24576, 512], P(('row', 'col')), may hold values from -6 to 6
- pattern_a: int32 [96, 2], replicated, may hold values 0 or 1
- orbitals_b: bfloat16 [24576, 512], P(('col', 'row')), may hold values from -6 to 6
- pattern_b: int32 [96, 2], replicated, may hold values 0 or 1
Outputs:
- induced_a: bfloat16 [24576, 512], P(('row', 'col'))
- induced_b: bfloat16 [24576, 512], P(('col', 'row'))
- orbital_margin: float32 [512, 512], replicated
The draws below stay inside these ranges and needn't reach their ends.
Inputs may be any that keep to these rules, and one draw needn't show every extreme that they name: margin_pattern[i, j] is 1 where block i of A and block j of B lie near each other in space, else 0.
All inputs are finite; a program needn't handle non-finite values.
Results may differ from the reference program's by a relative error of at most 0.0063.
Values may be sent and summed in bfloat16 or wider, within the bound.
A program may use at most 128 MiB of HBM per device.

```python
import math
import jax
import jax.numpy as jnp

BLK = 256
OCC = 512
N = 24576
NBLK = 96
OBLK = 2


def draw_margin_pattern(key, part):
    key = jax.random.fold_in(key, 7)
    first_key, second_key = jax.random.split(key)
    spots_a = jax.random.randint(first_key, (NBLK, 3), 0, 4)
    spots_b = jax.random.randint(second_key, (NBLK, 3), 0, 4)
    offsets = spots_a[:, None, :] - spots_b[None, :, :]
    distance = jnp.sum(offsets * offsets, axis=-1)
    return (distance <= 6).astype(jnp.int32)


def touch_ends(values, own_key, smallest, high):
    longest = values.shape.index(max(values.shape))
    spots = []
    for shift in (0, 1):
        where = [jax.random.randint(jax.random.fold_in(own_key, axis), (), 0, length) for axis, length in enumerate(values.shape)]
        where[longest] = (where[longest] + shift) % values.shape[longest]
        spots.append(tuple(where))
    return values.at[spots[0]].set(smallest).at[spots[1]].set(high)


def spiked(values, rng, source, target, blocks, factor):
    owner, partner = [(jnp.arange(values.shape[axis_at]) // (values.shape[axis_at] // blocks)).reshape([-1 if axis == axis_at else 1 for axis in range(values.ndim)]) for axis_at in (source, target)]
    chosen = jax.random.permutation(rng, blocks)[partner]
    strong = (owner == chosen) | (owner == (partner + blocks // 2) % blocks)
    return jnp.where(strong, factor * values, values)


def levels(stream_key, dims, cuts, smallest, largest):
    level, own = 1.0, jax.random.fold_in(stream_key, 6)
    for axis_at, shards_of in cuts:
        steps = jnp.exp(jax.random.uniform(jax.random.fold_in(own, axis_at), (shards_of,), jnp.float32, smallest / len(cuts), largest / len(cuts)))
        level = level * jnp.repeat(steps, dims[axis_at] // shards_of).reshape([-1 if axis == axis_at else 1 for axis in range(len(dims))])
    return level


def noise(own_key, extent, spread, reach, pieces=(), dtype=jnp.bfloat16):
    array = spread * jax.random.normal(own_key, extent, jnp.float32)
    if pieces:
        array = array * levels(own_key, extent, pieces, -0.22, 0.18)
    return jnp.clip(array, -reach, reach).astype(dtype)


def gaussian_with(rng, dims, spread, most, cuts, heavy, kind=jnp.bfloat16):
    result = spread * jax.random.normal(rng, dims, jnp.float32)
    if cuts:
        result = result * levels(rng, dims, cuts, -0.22, 0.18)
    return jnp.clip(spiked(result, jax.random.fold_in(rng, 3), *heavy), -most, most).astype(kind)


def setup_inputs(seed: int = 0) -> dict:
    key_list = jax.random.split(jax.random.key(seed), 7)
    return {
        "margin": gaussian_with(key_list[0], (N, N), N ** -0.5, 0.109375, ((0, 64), (1, 4)), (0, 1, 64, 4.0)),
        "margin_pattern": draw_margin_pattern(jax.random.fold_in(key_list[6], 71), 0),
        "orbitals_a": noise(key_list[2], (N, OCC), 1.0, 6.0, ((0, 256),)),
        "pattern_a": touch_ends((jax.random.randint(key_list[3], (NBLK, OBLK), 0, 4) < 3).astype(jnp.int32), jax.random.fold_in(key_list[3], 1), 0, 1),
        "orbitals_b": noise(key_list[4], (N, OCC), 1.0, 6.0, ((0, 256),)),
        "pattern_b": touch_ends((jax.random.randint(key_list[5], (NBLK, OBLK), 0, 4) < 3).astype(jnp.int32), jax.random.fold_in(key_list[5], 1), 0, 1),
    }


def mask_blocks(values, pattern, row_blocks, col_blocks):
    shaped = values.reshape(row_blocks, BLK, col_blocks, BLK)
    kept = shaped * pattern.astype(jnp.bfloat16)[:, None, :, None]
    return kept.reshape(row_blocks * BLK, col_blocks * BLK)

def reference(margin, margin_pattern, orbitals_a, pattern_a, orbitals_b, pattern_b):
    masked_margin = mask_blocks(margin, margin_pattern, NBLK, NBLK)
    masked_a = mask_blocks(orbitals_a, pattern_a, NBLK, OBLK)
    masked_b = mask_blocks(orbitals_b, pattern_b, NBLK, OBLK)
    b_image = jnp.dot(masked_margin, masked_b, preferred_element_type=jnp.float32).astype(jnp.bfloat16)
    a_image = jnp.dot(masked_margin.T, masked_a, preferred_element_type=jnp.float32).astype(jnp.bfloat16)
    orbital_margin = jnp.dot(masked_a.T, b_image, preferred_element_type=jnp.float32) * (1.0 / math.sqrt(N))
    rounded = orbital_margin.astype(jnp.bfloat16)
    factor = 1.0 / math.sqrt(OCC)
    induced_a = (jnp.dot(b_image, rounded.T, preferred_element_type=jnp.float32) * factor).astype(jnp.bfloat16)
    induced_b = (jnp.dot(a_image, rounded, preferred_element_type=jnp.float32) * factor).astype(jnp.bfloat16)
    return (induced_a, induced_b, orbital_margin)
```

```python
import math

import jax
import jax.numpy as jnp
from jax import lax
from jax.experimental import pallas as pl
from jax.experimental.pallas import tpu as pltpu
from jax.sharding import PartitionSpec as P

MESH = pl.DeviceIdType.MESH
F32 = jnp.float32
BF16 = jnp.bfloat16
BLK = 256
NX, NY, NZ = 4, 4, 8
CH = NX * NZ
LEN = ((4, 3), (4, 3), (3, 4), (3, 4), (4, 3))


def up(v, n):
    return lax.rem(v, n)


def contract0(a, b):
    return lax.dot_general(a, b, (((0,), (0,)), ((), ())), preferred_element_type=F32)


def kernel(
    m_ref, pm_ref, a_ref, pa_ref, b_ref, pb_ref,
    oa_ref, ob_ref, oo_ref,
    mbuf, afull, bbuf, bst, terms, zbuf, ubuf, xbuf, bacc, bpart, bslots,
    of32, obf, ar1, s2, ar2, ar3, rbuf, aimg, aother,
    lsem, msend, mrecv, asend, arecv, wsend, wrecv, gsend, grecv,
    rsend, zrecv, urecv, xrecv, bsend, brecv, osend1, orecv1, osend2, orecv2,
    osend3, orecv3, osend4, orecv4, dsend, drecv, ssend, srecv,
):
    r = lax.axis_index("row")
    y = lax.axis_index("col")
    x, z, c = r // (2 * NZ), (r // 2) % NZ, r % 2
    p = x * NZ + z

    def dev(dx, dz, dy, oc=None):
        core = c if oc is None else oc
        return (up(x + dx, NX) * (2 * NZ) + up(z + dz + NZ, NZ) * 2 + core, up(y + dy, NY))

    def chip(k, dz):
        return up(x + k, NX) * NZ + up(z + dz + NZ, NZ)

    def send(src, dst, ssem, rsem, to):
        pltpu.make_async_remote_copy(
            src_ref=src, dst_ref=dst, send_sem=ssem, recv_sem=rsem, device_id=to, device_id_type=MESH
        ).start()

    def got(dst, sem):
        pltpu.make_async_copy(dst, dst, sem).wait()

    other = 1 - c
    sib = dev(0, 0, 0, other)
    own_m = mbuf.at[pl.ds(pl.multiple_of(c * 384, 128), 384)]
    local = pltpu.make_async_copy(m_ref, own_m, lsem)
    local.start()

    def masked(ref, pat, d):
        first, last = (96 * d) // BLK, (96 * d + 95) // BLK
        rows = 96 * d + lax.broadcasted_iota(jnp.int32, (96, BLK), 0)
        inside = rows < (first + 1) * BLK
        parts = []
        for k in range(2):
            keep = jnp.where(inside, pat[first, k].astype(F32), pat[last, k].astype(F32))
            parts.append((ref[:, k * BLK:(k + 1) * BLK].astype(F32) * keep).astype(BF16))
        return parts

    arow = pl.multiple_of(384 * c + 96 * y, 16)
    a0, a1 = masked(a_ref, pa_ref, 4 * r + y)
    afull[pl.ds(arow, 96), 0:256] = a0
    afull[pl.ds(arow, 96), 256:512] = a1
    b0, b1 = masked(b_ref, pb_ref, 64 * y + r)
    here = jnp.where(c == 0, b0.astype(F32), b1.astype(F32)).astype(BF16)
    there = jnp.where(c == 0, b1.astype(F32), b0.astype(F32)).astype(BF16)
    brow = pl.multiple_of(96 * c, 16)
    for h in range(2):
        bbuf[h * CH + p, pl.ds(brow, 96), :] = here[:, h * 128:(h + 1) * 128]
        bst[h, :, :] = there[:, h * 128:(h + 1) * 128]

    partners = [sib]
    for dx in range(NX):
        for dy in range(NY):
            if dx or dy:
                partners.append(dev(dx, 0, dy))
    for dz in range(1, NZ):
        partners.append(dev(0, dz, 0))
    for dy in range(1, NY):
        partners.append(dev(0, 0, dy, other))
    bar = pltpu.get_barrier_semaphore()
    for to in partners:
        pl.semaphore_signal(bar, inc=1, device_id=to, device_id_type=MESH)
    pl.semaphore_wait(bar, len(partners))

    for h in range(2):
        piece = bbuf.at[h * CH + p, pl.ds(brow, 96)]
        send(bst.at[h], piece, wsend, wrecv.at[h], sib)
    own_a = afull.at[pl.ds(arow, 96)]
    for dy in range(NY):
        for oc in range(2):
            if dy or oc:
                to = dev(0, 0, dy, c if oc == 0 else other)
                send(own_a, own_a, asend, arecv.at[2 * dy + oc], to)
    send(m_ref, own_m, msend, mrecv, sib)

    def chunk(h, idx):
        return bbuf.at[h * CH + idx]

    def gsend_to(h, idx, to):
        send(chunk(h, idx), chunk(h, idx), gsend, grecv.at[h * CH + idx], to)

    def gwait(h, idx):
        got(chunk(h, idx), grecv.at[h * CH + idx])

    brow2 = pl.multiple_of(96 * other, 16)
    for h in range(2):
        got(bbuf.at[h * CH + p, pl.ds(brow2, 96)], wrecv.at[h])
    zup, zdown = dev(0, 1, 0), dev(0, -1, 0)
    for k in (1, 3, 2):
        gsend_to(0, p, dev(k, 0, 0))
    gsend_to(0, p, zup)
    gsend_to(0, p, zdown)
    gsend_to(1, p, zup)
    gsend_to(1, p, zdown)
    for k in (1, 3, 2):
        gsend_to(1, p, dev(k, 0, 0))
    for k in (1, 3, 2):
        gwait(0, chip(k, 0))
        gsend_to(0, chip(k, 0), zup)
        gsend_to(0, chip(k, 0), zdown)

    def gather_step(s):
        for k in (0, 4, 1, 3, 2):
            h, kk = (1, 0) if k == 4 else (0, k)
            for way, (lim, sign, to) in enumerate(((LEN[k][0], -1, zup), (LEN[k][1], 1, zdown))):
                if s <= lim:
                    idx = chip(kk, sign * s)
                    gwait(h, idx)
                    if s < lim:
                        gsend_to(h, idx, to)
                    if h == 1:
                        for kx in (1, 3, 2):
                            gsend_to(1, idx, dev(kx, 0, 0))

    ccol = pl.multiple_of(c * BLK, BLK)

    def term_body(q, carry):
        cols = pl.ds(pl.multiple_of(q * 384, 128), 384)
        strips = []
        for i in range(3):
            rows = pl.ds(i * BLK, BLK)
            strip = []
            for j in range(3):
                keep = pm_ref[3 * p + i, 24 * y + (3 * q + j) // 2].astype(F32)
                sub = pl.ds(pl.multiple_of(q * 384 + j * 128, 128), 128)
                tile = mbuf[rows, sub] * jnp.full((BLK, 128), keep, F32).astype(BF16)
                mbuf[rows, sub] = tile
                strip.append(tile)
            strips.append(jnp.concatenate(strip, axis=1))
        tile = jnp.concatenate(strips, axis=0)
        res = contract0(tile, afull[:, pl.ds(ccol, BLK)])
        for e in range(2):
            for h in range(2):
                terms[h * CH + 2 * q + e] = res[192 * e:192 * e + 192, 128 * h:128 * h + 128].astype(BF16)
        return carry

    gather_step(1)
    for dy in range(NY):
        for oc in range(2):
            if dy or oc:
                core = c if oc == 0 else other
                row = pl.multiple_of(384 * core + 96 * up(y - dy + NY, NY), 16)
                got(afull.at[pl.ds(row, 96)], arecv.at[2 * dy + oc])
    local.wait()
    got(mbuf.at[pl.ds(pl.multiple_of(other * 384, 128), 384)], mrecv)
    lax.fori_loop(0, 5, term_body, 0)
    gather_step(2)
    lax.fori_loop(5, 11, term_body, 0)
    gather_step(3)
    lax.fori_loop(11, 16, term_body, 0)
    gather_step(4)

    def t_at(h, idx):
        return terms.at[h * CH + idx]

    order = (4, -3, 3, -2, 2, -1, 1, 0)

    def usend(i):
        for k in (1, 3, 2):
            send(t_at(1, chip(k, order[i])), ubuf.at[3 * i + k - 1], rsend, urecv.at[3 * i + k - 1], dev(k, 0, 0))

    def usum(i):
        total = terms[CH + chip(0, order[i])].astype(F32)
        for k in (1, 3, 2):
            got(ubuf.at[3 * i + k - 1], urecv.at[3 * i + k - 1])
            total += ubuf[3 * i + k - 1].astype(F32)
        return total

    def zslot(k, way, s):
        return (2 * k + way) * 4 + s

    def zsend(src, k, way, s):
        send(src, zbuf.at[zslot(k, way, s)], rsend, zrecv.at[zslot(k, way, s)], zup if way == 0 else zdown)

    def scatter_step(s):
        for k in range(4):
            for way in range(2):
                lim = LEN[k][way]
                if s < lim:
                    idx = chip(k, (lim - s) if way == 0 else (s - lim))
                    if s == 0:
                        zsend(t_at(0, idx), k, way, 0)
                    else:
                        slot = zslot(k, way, s - 1)
                        got(zbuf.at[slot], zrecv.at[slot])
                        zbuf[slot] = (zbuf[slot].astype(F32) + terms[idx].astype(F32)).astype(BF16)
                        zsend(zbuf.at[slot], k, way, s)

    def scatter_step1(s):
        for way in range(2):
            lim = LEN[4][way]
            if s < lim:
                off = (lim - s) if way == 0 else (s - lim)
                total = usum(order.index(off))
                if s > 0:
                    slot = zslot(4, way, s - 1)
                    got(zbuf.at[slot], zrecv.at[slot])
                    total += zbuf[slot].astype(F32)
                first = 3 * order.index(off)
                ubuf[first] = total.astype(BF16)
                zsend(ubuf.at[first], 4, way, s)

    def b_body(g, carry):
        cols = pl.ds(pl.multiple_of(g * 768, 128), 768)
        halves = [bbuf[pl.ds(h * CH + 4 * g, 4)].reshape(768, 128) for h in range(2)]
        bacc[...] += jnp.dot(mbuf[:, cols], jnp.concatenate(halves, axis=1), preferred_element_type=F32)
        return carry

    usend(0)
    scatter_step(0)
    usend(1)
    usend(2)
    for i in range(8):
        for k in (1, 3, 2):
            gwait(1, chip(k, order[i]))
    bacc[...] = jnp.zeros_like(bacc)
    lax.fori_loop(0, 4, b_body, 0)
    scatter_step(1)
    usend(3)
    usend(4)
    scatter_step1(0)
    lax.fori_loop(4, 8, b_body, 0)
    bpart[...] = bacc[...].astype(BF16).reshape(2, NY, 96, BLK)
    for dy in range(NY):
        for oc in range(2):
            if dy or oc:
                core = c if oc == 0 else other
                slot = 2 * dy + oc
                send(bpart.at[core, up(y + dy, NY)], bslots.at[slot], bsend, brecv.at[slot], dev(0, 0, dy, core))
    bslots[0] = bpart[c, y]
    orb = contract0(afull[...], bpart[...].reshape(768, BLK)).reshape(16, 32, BLK)
    of32[...] = orb
    obf[...] = orb.astype(BF16)
    for dx in range(NX):
        for dy in range(NY):
            if dx or dy:
                slot = 4 * dx + dy
                send(obf.at[up(x + dx, NX) * 4 + up(y + dy, NY)], ar1.at[slot], osend1, orecv1.at[slot], dev(dx, 0, dy))
    scatter_step(2)
    usend(5)
    usend(6)
    scatter_step1(1)
    total = of32[4 * x + y]
    for slot in range(1, 16):
        got(ar1.at[slot], orecv1.at[slot])
        total += ar1[slot].astype(F32)
    for e in range(8):
        s2[e] = total[8 * (e // 2):8 * (e // 2) + 8, 128 * (e % 2):128 * (e % 2) + 128]
    for dz in range(1, NZ):
        send(s2.at[up(z + dz, NZ)], ar2.at[dz], osend2, orecv2.at[dz], dev(0, dz, 0))
    scatter_step(3)
    usend(7)
    scatter_step1(2)
    total = s2[z]
    for dz in range(1, NZ):
        got(ar2.at[dz], orecv2.at[dz])
        total += ar2[dz]
    ar3[z] = total * (1.0 / math.sqrt(24576))
    for dz in range(1, NZ):
        send(ar3.at[z], ar3.at[z], osend3, orecv3.at[dz], dev(0, dz, 0))
    scatter_step1(3)

    def zlast(k):
        total = terms[CH * (k == 4) + chip(k % 4, 0)].astype(F32) if k < 4 else usum(7)
        for way in range(2):
            slot = zslot(k, way, LEN[k][way] - 1)
            got(zbuf.at[slot], zrecv.at[slot])
            total += zbuf[slot].astype(F32)
        return total

    for k in (1, 3, 2):
        xbuf[k] = zlast(k).astype(BF16)
        send(xbuf.at[k], xbuf.at[3 + k], rsend, xrecv.at[k], dev(k, 0, 0))
    for dz in range(1, NZ):
        src = up(z - dz + NZ, NZ)
        got(ar3.at[src], orecv3.at[dz])
    piece = jnp.concatenate(
        [jnp.concatenate([ar3[2 * g], ar3[2 * g + 1]], axis=1) for g in range(4)], axis=0
    )
    rbuf[c, 4 * x + y] = piece.astype(BF16)
    for dx in range(NX):
        for dy in range(NY):
            if dx or dy:
                slot = 4 * dx + dy
                mine = rbuf.at[c, 4 * x + y]
                send(mine, mine, osend4, orecv4.at[slot], dev(dx, 0, dy))
    half0 = zlast(0)
    half1 = zlast(4)
    parts = [bslots[0].astype(F32), None]
    for dy in range(NY):
        for oc in range(2):
            slot = 2 * dy + oc
            if slot:
                got(bslots.at[slot], brecv.at[slot])
                v = bslots[slot].astype(F32)
                parts[oc] = v if parts[oc] is None else parts[oc] + v
    b_here, b_there = parts[0].astype(BF16), parts[1].astype(BF16)
    for k in (1, 3, 2):
        got(xbuf.at[3 + k], xrecv.at[k])
        half0 += xbuf[3 + k].astype(F32)
    aimg[:, 0:128] = half0.astype(BF16)
    aimg[:, 128:256] = half1.astype(BF16)
    send(aimg.at[pl.ds(brow2, 96)], aother, ssend, srecv, sib)
    for dx in range(NX):
        for dy in range(NY):
            if dx or dy:
                slot = 4 * dx + dy
                idx = up(x - dx + NX, NX) * 4 + up(y - dy + NY, NY)
                got(rbuf.at[c, idx], orecv4.at[slot])
    send(rbuf.at[c], rbuf.at[c], dsend, drecv, sib)
    factor = 1.0 / math.sqrt(512)

    def dot_t(a, b):
        return lax.dot_general(a, b, (((1,), (1,)), ((), ())), preferred_element_type=F32)

    def half_r(h):
        return rbuf[h].reshape(512, BLK)

    res_a = dot_t(b_here, half_r(c))
    got(aother, srecv)
    got(rbuf.at[other], drecv)
    res_a += dot_t(b_there, half_r(other))
    oa_ref[...] = (res_a * factor).astype(BF16)
    mine = aimg[pl.ds(brow, 96), :]
    theirs = aother[...]
    is0 = c == 0
    left = jnp.where(is0, mine.astype(F32), theirs.astype(F32)).astype(BF16)
    right = jnp.where(is0, theirs.astype(F32), mine.astype(F32)).astype(BF16)
    whole = jnp.concatenate([left, right], axis=1)
    for h in range(2):
        ob_ref[:, h * BLK:(h + 1) * BLK] = (
            jnp.dot(whole, half_r(h), preferred_element_type=F32) * factor
        ).astype(BF16)
        oo_ref[:, h * BLK:(h + 1) * BLK] = half_r(h).astype(F32)

    got(bst, wsend)
    got(afull.at[pl.ds(0, 672)], asend)
    pltpu.make_async_copy(m_ref, own_m, msend).wait()
    got(bbuf.at[pl.ds(0, 62)], gsend)
    got(bbuf.at[pl.ds(0, 62)], rsend)
    got(bslots.at[pl.ds(1, 7)], bsend)
    got(obf.at[pl.ds(0, 15)], osend1)
    got(ar2.at[pl.ds(1, 7)], osend2)
    got(ar2.at[pl.ds(1, 7)], osend3)
    got(obf.at[pl.ds(0, 15)], osend4)
    got(rbuf.at[c], dsend)
    got(aother, ssend)


def local(margin, margin_pattern, orbitals_a, pattern_a, orbitals_b, pattern_b):
    vmem, smem, any_ = (pl.BlockSpec(memory_space=s) for s in (pltpu.VMEM, pltpu.SMEM, pl.ANY))
    dma = pltpu.SemaphoreType.DMA

    def buf(*shape, dtype=BF16):
        return pltpu.VMEM(shape, dtype)

    return pl.pallas_call(
        kernel,
        out_shape=(
            jax.ShapeDtypeStruct((96, 512), BF16),
            jax.ShapeDtypeStruct((96, 512), BF16),
            jax.ShapeDtypeStruct((512, 512), F32),
        ),
        in_specs=[any_, smem, vmem, smem, vmem, smem],
        out_specs=(vmem, vmem, vmem),
        scratch_shapes=[
            buf(768, 6144), buf(768, 512), buf(64, 192, 128), buf(2, 96, 128), buf(64, 192, 128),
            buf(40, 192, 128), buf(24, 192, 128), buf(7, 192, 128),
            buf(768, 256, dtype=F32), buf(2, 4, 96, 256), buf(8, 96, 256),
            buf(16, 32, 256, dtype=F32), buf(16, 32, 256), buf(16, 32, 256),
            buf(8, 8, 128, dtype=F32), buf(8, 8, 128, dtype=F32), buf(8, 8, 128, dtype=F32),
            buf(2, 16, 32, 256), buf(192, 256), buf(96, 256),
            dma, dma, dma, dma, dma((8,)), dma, dma((2,)), dma, dma((64,)),
            dma, dma((40,)), dma((24,)), dma((4,)), dma, dma((8,)), dma, dma((16,)), dma, dma((8,)),
            dma, dma((8,)), dma, dma((16,)), dma, dma, dma, dma,
        ],
        compiler_params=pltpu.CompilerParams(
            collective_id=0, has_side_effects=True, vmem_limit_bytes=48 << 20
        ),
        name="exchange",
    )(margin, margin_pattern, orbitals_a, pattern_a, orbitals_b, pattern_b)


def solution(mesh):
    in_specs = (P("row", "col"), P(), P(("row", "col"), None), P(), P(("col", "row"), None), P())
    out_specs = (P(("row", "col"), None), P(("col", "row"), None), P())
    return jax.shard_map(local, mesh=mesh, in_specs=in_specs, out_specs=out_specs, check_vma=False)
```

```python
import math

import jax
import jax.numpy as jnp
from jax import lax
from jax.experimental import pallas as pl
from jax.experimental.pallas import tpu as pltpu
from jax.sharding import PartitionSpec as P

MESH = pl.DeviceIdType.MESH
F32 = jnp.float32
BF16 = jnp.bfloat16
BLK = 256
NX, NY, NZ = 4, 4, 8
CH = NX * NZ
PART = ((0, 160), (160, 224))
LEN = ((4, 3), (4, 3), (3, 4), (3, 4), (4, 3))

ORDER = (
    ("x0", 1), ("x0", 3), ("z1", 0, 1), ("z1", 1, 1), ("x0", 2), ("apass",), ("x1", 0), ("z0", 0, 0, 1),
    ("z0", 0, 1, 1), ("z0", 1, 0, 1), ("z0", 1, 1, 1), ("aturn",), ("x1", -1), ("terms", 0), ("z1", 0, 2),
    ("z1", 1, 2), ("x1", 1), ("z0", 3, 0, 1), ("z0", 2, 1, 1), ("terms", 1), ("z0", 0, 0, 2), ("z0", 0, 1, 2),
    ("z0", 2, 0, 1), ("terms", 2), ("z0", 1, 0, 2), ("z0", 1, 1, 2), ("z0", 3, 1, 1), ("terms", 3), ("z1", 0, 3),
    ("z1", 1, 3), ("x1", -2), ("x1", 2), ("z0", 2, 1, 2), ("z0", 0, 0, 3), ("z0", 0, 1, 3), ("z0", 3, 0, 2),
    ("bpart", 0), ("z0", 1, 1, 3), ("z0", 2, 0, 2), ("z0", 3, 1, 2), ("z0", 1, 0, 3), ("x1", -3), ("z1", 0, 4),
    ("z0", 2, 1, 3), ("r0", 0, 0, 0), ("r0", 0, 1, 0), ("r0", 1, 0, 0), ("r0", 1, 1, 0), ("u", 4), ("x1", 3),
    ("r0", 2, 0, 0), ("r0", 2, 1, 0), ("r0", 3, 0, 0), ("r0", 3, 1, 0), ("z0", 0, 0, 4), ("z0", 1, 0, 4),
    ("z0", 2, 0, 3), ("z0", 3, 0, 3), ("u", -3), ("z0", 2, 1, 4), ("z0", 3, 1, 3), ("bpart", 1), ("r0", 0, 0, 1),
    ("x1", -4), ("u", 3), ("r0", 0, 1, 1), ("r0", 1, 0, 1), ("r0", 1, 1, 1), ("u", -2), ("r0", 2, 0, 1),
    ("r0", 2, 1, 1), ("r0", 3, 0, 1), ("r0", 3, 1, 1), ("upass", 4), ("bpart", 2), ("z0", 3, 1, 4), ("r0", 0, 0, 2),
    ("u", 2), ("bpart", 3), ("orb",), ("r0", 0, 1, 2), ("r0", 1, 0, 2), ("r0", 1, 1, 2), ("r0", 2, 0, 2),
    ("r0", 2, 1, 2), ("r0", 3, 0, 2), ("r0", 3, 1, 2), ("r0", 0, 0, 3), ("r1", 0, 0), ("upass", -3), ("upass", 3),
    ("r0", 1, 0, 3), ("upass", -2), ("upass", 2), ("u", -1), ("r0", 2, 1, 3), ("r0", 3, 1, 3), ("u", 1), ("r1", 1, 0),
    ("orb2",), ("u", 0), ("r1", 0, 1), ("r0x", 1), ("r0x", 2), ("r0x", 3), ("upass", -1), ("upass", 1), ("r1", 1, 1),
    ("upass", 0), ("r1", 0, 2), ("orb4",), ("r1", 1, 2), ("end0",), ("r1", 0, 3), ("orbend",), ("end1",),
)


def up(v, n):
    return lax.rem(v, n)


def contract0(a, b):
    return lax.dot_general(a, b, (((0,), (0,)), ((), ())), preferred_element_type=F32)


def split(v):
    high = v.astype(BF16)
    return high, (v - high.astype(F32)).astype(BF16)


def kernel(
    m_ref, pm_hbm, a_hbm, pa_ref, b_hbm, pb_ref,
    r_out, b_out, a_out,
    mbuf, afull, at, bbuf, bst, terms, zbuf, zbuf1, ubuf, xbuf, bacc, bpart, bslots,
    of32, obf, ar1, az, rbuf, aimg, aother, bwhole, awhole, a_ref, b_ref, pm_ref,
    lsem, insem, msend, mrecv, asend, arecv, wsend, wrecv, gsend, grecv,
    rsend, zrecv, urecv, xrecv, bsend, brecv, osend1, orecv1, osend2, orecv2,
    osend4, orecv4, dsend, drecv, ssend, srecv, outsem,
):
    r = lax.axis_index("row")
    y = lax.axis_index("col")
    x, z, c = r // (2 * NZ), (r // 2) % NZ, r % 2
    p = x * NZ + z

    def dev(dx, dz, dy, oc=None):
        core = c if oc is None else oc
        return (up(x + dx, NX) * (2 * NZ) + up(z + dz + NZ, NZ) * 2 + core, up(y + dy, NY))

    def chip(k, dz):
        return up(x + k, NX) * NZ + up(z + dz + NZ, NZ)

    def send(src, dst, ssem, rsem, to):
        pltpu.make_async_remote_copy(
            src_ref=src, dst_ref=dst, send_sem=ssem, recv_sem=rsem, device_id=to, device_id_type=MESH
        ).start()

    def got(dst, sem):
        pltpu.make_async_copy(dst, dst, sem).wait()

    other = 1 - c
    sib = dev(0, 0, 0, other)
    zup, zdown = dev(0, 1, 0), dev(0, -1, 0)

    partners = [sib, zup, zdown] + [dev(k, 0, 0) for k in (1, 2, 3)] + [dev(0, 0, k) for k in (1, 2, 3)]
    bar = pltpu.get_barrier_semaphore()
    for to in partners:
        pl.semaphore_signal(bar, inc=1, device_id=to, device_id_type=MESH)
    loads = []
    for i, (src, dst) in enumerate(((b_hbm, b_ref), (a_hbm, a_ref), (pm_hbm, pm_ref))):
        loads.append(pltpu.make_async_copy(src, dst, insem.at[i]))
        loads[-1].start()
    own_m = mbuf.at[pl.ds(pl.multiple_of(c * 384, 128), 384)]
    local = pltpu.make_async_copy(m_ref, own_m, lsem)
    local.start()

    def masked(ref, pat, d):
        first, last = (96 * d) // BLK, (96 * d + 95) // BLK
        rows = 96 * d + lax.broadcasted_iota(jnp.int32, (96, BLK), 0)
        inside = rows < (first + 1) * BLK
        parts = []
        for k in range(2):
            keep = jnp.where(inside, pat[k, first].astype(F32), pat[k, last].astype(F32))
            parts.append((ref[:, k * BLK:(k + 1) * BLK].astype(F32) * keep).astype(BF16))
        return parts

    loads[0].wait()
    b0, b1 = masked(b_ref, pb_ref, 64 * y + r)
    here = jnp.where(c == 0, b0.astype(F32), b1.astype(F32)).astype(BF16)
    there = jnp.where(c == 0, b1.astype(F32), b0.astype(F32)).astype(BF16)
    brow = pl.multiple_of(96 * c, 16)
    for h in range(2):
        bbuf[p, pl.ds(pl.multiple_of(192 * h + 96 * c, 16), 96), :] = here[:, h * 128:(h + 1) * 128]
        bst[h, :, :] = there[:, h * 128:(h + 1) * 128]

    loads[1].wait()
    arow = pl.multiple_of(384 * c + 96 * y, 16)
    a0, a1 = masked(a_ref, pa_ref, 4 * r + y)
    afull[pl.ds(arow, 96), 0:256] = a0
    afull[pl.ds(arow, 96), 256:512] = a1
    pl.semaphore_wait(bar, len(partners))

    for h in range(2):
        piece = bbuf.at[p, pl.ds(pl.multiple_of(192 * h + 96 * c, 16), 96)]
        send(bst.at[h], piece, wsend, wrecv.at[h], sib)
    def a_rows(core, dy):
        return afull.at[pl.ds(pl.multiple_of(384 * core + 96 * up(y + NY - dy, NY), 16), 96)]

    own_a = a_rows(c, 0)
    send(own_a, own_a, asend, arecv.at[4], sib)
    for dy in (1, 3, 2):
        send(own_a, own_a, asend, arecv.at[dy], dev(0, 0, dy))

    def margin_piece(i):
        def body(t, carry):
            j = 6 * i + t
            cols = pl.ds(pl.multiple_of(BLK * j, BLK), BLK)
            for e in range(3):
                rows = pl.ds(pl.multiple_of(384 * c + 128 * e, 128), 128)
                keep = pm_ref[3 * p + (3 * c + e) // 2, 24 * y + j].astype(F32)
                mbuf[rows, cols] = mbuf[rows, cols] * jnp.full((128, BLK), keep, F32).astype(BF16)
            return carry

        lax.fori_loop(0, 6, body, 0)
        piece = mbuf.at[pl.ds(pl.multiple_of(384 * c, 128), 384), pl.ds(1536 * i, 1536)]
        send(piece, piece, msend, mrecv.at[i], sib)

    local.wait()
    loads[2].wait()
    margin_piece(0)
    margin_piece(1)

    def chunk(h, idx):
        return bbuf.at[idx, pl.ds(*PART[h])]

    def gsend_to(h, idx, to):
        send(chunk(h, idx), chunk(h, idx), gsend, grecv.at[h * CH + idx], to)

    def gwait(h, idx):
        got(chunk(h, idx), grecv.at[h * CH + idx])

    brow2 = pl.multiple_of(96 * other, 16)
    for h in range(2):
        got(bbuf.at[p, pl.ds(pl.multiple_of(192 * h + 96 * other, 16), 96)], wrecv.at[h])
    for k in (1, 3, 2):
        gsend_to(0, p, dev(k, 0, 0))
    gsend_to(1, p, zup)
    gsend_to(1, p, zdown)
    gsend_to(0, p, zup)
    gsend_to(0, p, zdown)
    for k in (1, 3):
        gsend_to(1, p, dev(k, 0, 0))
    margin_piece(2)
    margin_piece(3)

    def do_x0(k):
        gwait(0, chip(k, 0))
        gsend_to(0, chip(k, 0), zup)
        gsend_to(0, chip(k, 0), zdown)

    def do_z0(k, way, s):
        idx = chip(k, s if way else -s)
        gwait(0, idx)
        if s < LEN[k][way]:
            gsend_to(0, idx, zdown if way else zup)

    def do_z1(way, s):
        idx = chip(0, s if way else -s)
        gwait(1, idx)
        if s < LEN[4][way]:
            gsend_to(1, idx, zdown if way else zup)
        for k in (1, 3):
            gsend_to(1, idx, dev(k, 0, 0))

    def offsets(s):
        return (0,) if s == 0 else (-s, s) if s < 4 else (-s,)

    def do_x1(off):
        odd_chunk = (z + off + NZ) % 2
        gwait(1, chip(1, off))
        gwait(1, chip(3, off))
        gsend_to(1, chip(3 - 2 * odd_chunk, off), dev(1 + 2 * odd_chunk, 0, 0))

    def gather_last(s):
        for off in offsets(s):
            gwait(1, chip(2, off))

    ccol = pl.multiple_of(c * BLK, BLK)

    def term_body(q, carry):
        cols = pl.ds(pl.multiple_of(q * 768, 128), 768)
        both = jnp.dot(at[pl.ds(ccol, BLK), :], mbuf[:, cols], preferred_element_type=F32)
        low_lanes = lax.broadcasted_iota(jnp.int32, (64, 128), 1) < 64
        for u in range(4):
            h, pair = u % 2, u // 2
            whole = both[128 * h:128 * h + 128, 384 * pair:384 * pair + 384]
            top, bottom = whole[0:64, 128:256], whole[64:128, 128:256]
            first = jnp.where(low_lanes, top, pltpu.roll(bottom, 64, 1))
            second = jnp.where(low_lanes, pltpu.roll(top, 64, 1), bottom)
            for e, (tile_e, rest) in enumerate(((whole[:, 0:128], first), (whole[:, 256:384], second))):
                chunk_at = 4 * q + 2 * pair + e
                terms[chunk_at, 192 * h:192 * h + 128, :] = tile_e.astype(BF16)
                terms[chunk_at, 192 * h + 128:192 * h + 192, :] = rest.astype(BF16)
        return carry

    halfz, odd = z // 2, z % 2

    def do_terms(i):
        if i == 0:
            for j in range(4):
                got(mbuf.at[pl.ds(pl.multiple_of(384 * other, 128), 384), pl.ds(1536 * j, 1536)], mrecv.at[j])
        lax.fori_loop(2 * i, 2 * i + 2, term_body, 0)

    def do_bpart(i):
        if i == 0:
            gather_last(0)
        gather_last(i + 1)
        shift = (0, 3 + 2 * odd, 1 + 2 * odd, 2)[i]
        pair = up(halfz + shift, NZ // 2)
        tiles, rows = [], []
        for k in range(NX):
            first = up(x + k, NX) * NZ + 2 * pair
            tiles.append(mbuf[:, pl.ds(pl.multiple_of(192 * first, 128), 384)])
            halves = [bbuf[pl.ds(first, 2), 192 * h:192 * h + 192, :].reshape(384, 128) for h in range(2)]
            rows.append(jnp.concatenate(halves, axis=1))
        part = jnp.dot(
            jnp.concatenate(tiles, axis=1), jnp.concatenate(rows, axis=0), preferred_element_type=F32
        )
        bacc[...] = part if i == 0 else bacc[...] + part

    def do_apass():
        for dy in (1, 3, 2):
            got(a_rows(c, dy), arecv.at[dy])
            send(a_rows(c, dy), a_rows(c, dy), asend, arecv.at[4 + dy], sib)

    def do_aturn():
        for dy in (0, 1, 3, 2):
            got(a_rows(other, dy), arecv.at[4 + dy])
        at[...] = afull[...].T

    def t_at(h, idx):
        return terms.at[idx, pl.ds(*PART[h])]

    def t_val(h, idx):
        return terms[idx, pl.ds(*PART[h]), :].astype(F32)

    order = (4, -3, 3, -2, 2, -1, 1, 0)

    def ways(off):
        odd_chunk = (z + off + NZ) % 2
        return 1 + 2 * odd_chunk, 3 - 2 * odd_chunk

    def do_u(off):
        i = 3 * order.index(off)
        ahead, back = ways(off)
        send(t_at(1, chip(2, off)), ubuf.at[i], rsend, urecv.at[i], dev(ahead, 0, 0))
        send(t_at(1, chip(back, off)), ubuf.at[i + 1], rsend, urecv.at[i + 1], dev(back, 0, 0))

    def do_upass(off):
        i = 3 * order.index(off)
        ahead, _ = ways(off)
        got(ubuf.at[i], urecv.at[i])
        ubuf[i] = (ubuf[i].astype(F32) + t_val(1, chip(ahead, off))).astype(BF16)
        send(ubuf.at[i], ubuf.at[i + 2], rsend, urecv.at[i + 2], dev(ahead, 0, 0))

    def usum(off):
        total = t_val(1, chip(0, off))
        i = 3 * order.index(off)
        for j in (i + 1, i + 2):
            got(ubuf.at[j], urecv.at[j])
            total += ubuf[j].astype(F32)
        return total

    def zref(k, way, s):
        if k == 4:
            return zbuf1.at[4 * way + s], zrecv.at[32 + 4 * way + s]
        slot = 8 * k + 4 * way + s
        return zbuf.at[slot], zrecv.at[slot]

    def zsend(src, k, way, s):
        dst, sem = zref(k, way, s)
        send(src, dst, rsend, sem, zup if way == 0 else zdown)

    def do_r0(k, way, s):
        lim = LEN[k][way]
        idx = chip(k, (s - lim) if way else (lim - s))
        if s == 0:
            zsend(t_at(0, idx), k, way, 0)
        else:
            ref, sem = zref(k, way, s - 1)
            got(ref, sem)
            ref[...] = (ref[...].astype(F32) + t_val(0, idx)).astype(BF16)
            zsend(ref, k, way, s)

    def do_r1(way, s):
        lim = LEN[4][way]
        off = (s - lim) if way else (lim - s)
        total = usum(off)
        if s > 0:
            ref, sem = zref(4, way, s - 1)
            got(ref, sem)
            total += ref[...].astype(F32)
        mine = ubuf.at[3 * order.index(off) + 1]
        mine[...] = total.astype(BF16)
        zsend(mine, 4, way, s)

    def plane():
        return [(4 * dx + dy, dx, dy) for dx in range(NX) for dy in range(NY) if dx or dy]

    def do_orb():
        b_all = bacc[...]
        high = b_all.astype(BF16)
        low = (b_all - high.astype(F32)).astype(BF16)
        bpart[...] = high.reshape(2, NY, 96, BLK)
        orb = jnp.dot(at[...], high, preferred_element_type=F32)
        orb += jnp.dot(at[...], low, preferred_element_type=F32)
        orb = orb.reshape(16, 32, BLK)
        of32[...] = orb
        obf[...] = orb.astype(BF16)
        for slot, dx, dy in plane():
            src = obf.at[up(x + dx, NX) * 4 + up(y + dy, NY)]
            send(src, ar1.at[slot], osend1, orecv1.at[slot], dev(dx, 0, dy))
        for dy in range(NY):
            for oc in range(2):
                if dy or oc:
                    core = c if oc == 0 else other
                    slot = 2 * dy + oc
                    src = bpart.at[core, up(y + dy, NY)]
                    send(src, bslots.at[slot], bsend, brecv.at[slot], dev(0, 0, dy, core))
        bslots[0] = bpart[c, y]

    def do_orb2():
        total = of32[4 * x + y]
        for slot, _, _ in plane():
            got(ar1.at[slot], orecv1.at[slot])
            total += ar1[slot].astype(F32)
        az[z] = total.astype(BF16)
        for dz in (4, 3, 5, 2, 6, 1, 7):
            send(az.at[z], az.at[z], osend2, orecv2.at[dz], dev(0, dz, 0))

    def do_orb4():
        for dz in range(1, NZ):
            got(az.at[up(z - dz + NZ, NZ)], orecv2.at[dz])
        total = az[0].astype(F32)
        for i in range(1, NZ):
            total += az[i].astype(F32)
        mine = rbuf.at[c, 4 * x + y]
        mine[...] = (total * (1.0 / math.sqrt(24576))).astype(BF16)
        for slot, dx, dy in plane():
            send(mine, mine, osend4, orecv4.at[slot], dev(dx, 0, dy))

    def zlast(k):
        total = t_val(0, chip(k, 0)) if k < 4 else usum(0)
        for way in range(2):
            ref, sem = zref(k, way, LEN[k][way] - 1)
            got(ref, sem)
            total += ref[...].astype(F32)
        return total

    def do_r0x(k):
        xbuf[k] = zlast(k).astype(BF16)
        send(xbuf.at[k], xbuf.at[3 + k], rsend, xrecv.at[k], dev(k, 0, 0))

    halves = []

    def do_end0():
        total = zlast(0)
        for k in (1, 3, 2):
            got(xbuf.at[3 + k], xrecv.at[k])
            total += xbuf[3 + k].astype(F32)
        halves.append(total)
        for oc in range(2):
            total = 0.0
            for dy in range(NY):
                slot = 2 * dy + oc
                if slot:
                    got(bslots.at[slot], brecv.at[slot])
                total += bslots[slot].astype(F32)
            bwhole[c if oc == 0 else other] = total
        pltpu.make_async_copy(bwhole, b_out, outsem.at[0]).start()

    def do_end1():
        halves.append(zlast(4))

    def do_orbend():
        for slot, dx, dy in plane():
            got(rbuf.at[c, up(x - dx + NX, NX) * 4 + up(y - dy + NY, NY)], orecv4.at[slot])
        send(rbuf.at[c], rbuf.at[c], dsend, drecv, sib)

    steps = dict(
        x0=do_x0, z0=do_z0, z1=do_z1, x1=do_x1, apass=do_apass, aturn=do_aturn, terms=do_terms, bpart=do_bpart,
        u=do_u, upass=do_upass, r0=do_r0, r1=do_r1, r0x=do_r0x, orb=do_orb, orb2=do_orb2, orb4=do_orb4,
        orbend=do_orbend, end0=do_end0, end1=do_end1,
    )
    for name, *where in ORDER:
        steps[name](*where)

    image = jnp.concatenate(halves, axis=0)
    for h in range(2):
        lanes = pl.ds(128 * h, 128)
        packed = image[192 * h + 128:192 * h + 192, :]
        rest = jnp.concatenate([packed, pltpu.roll(packed, 64, 1)], axis=0).T
        aimg[pl.ds(pl.multiple_of(64 * odd, 8), 128), lanes] = image[192 * h:192 * h + 128, :].T
        aimg[pl.ds(pl.multiple_of(128 * (1 - odd), 8), 64), lanes] = rest[0:64, :]
    send(aimg.at[pl.ds(pl.multiple_of(96 * other, 8), 96)], aother, ssend, srecv, sib)
    got(rbuf.at[other], drecv)
    pltpu.make_async_copy(rbuf, r_out, outsem.at[1]).start()
    awhole[c] = aimg[pl.ds(brow, 96), :]
    got(aother, srecv)
    awhole[other] = aother[...]
    pltpu.make_async_copy(awhole, a_out, outsem.at[2]).start()

    for i, (src, dst) in enumerate(((bwhole, b_out), (rbuf, r_out), (awhole, a_out))):
        pltpu.make_async_copy(src, dst, outsem.at[i]).wait()
    got(bst, wsend)
    got(afull.at[pl.ds(0, 672)], asend)
    got(own_m, msend)
    got(bbuf.at[pl.ds(0, 31)], gsend)
    got(bbuf.at[pl.ds(0, 31)], rsend)
    got(bslots.at[pl.ds(1, 7)], bsend)
    got(obf.at[pl.ds(0, 15)], osend1)
    got(obf.at[pl.ds(0, 7)], osend2)
    got(obf.at[pl.ds(0, 15)], osend4)
    got(rbuf.at[c], dsend)
    got(aother, ssend)


def last_kernel(r_ref, b_ref, a_ref, oa_ref, ob_ref, oo_ref):
    factor = 1.0 / math.sqrt(512)
    res_a, res_b = 0.0, [0.0, 0.0]
    for h in range(2):
        oo_ref[:, h * BLK:(h + 1) * BLK] = r_ref[h].reshape(512, BLK).astype(F32)
    for h in range(2):
        half = r_ref[h].reshape(512, BLK)
        for v in split(b_ref[h]):
            res_a += lax.dot_general(v, half, (((1,), (1,)), ((), ())), preferred_element_type=F32)
        for v in split(a_ref[h]):
            for j in range(2):
                rows = r_ref[j, 8 * h:8 * h + 8].reshape(BLK, BLK)
                res_b[j] += jnp.dot(v, rows, preferred_element_type=F32)
    oa_ref[...] = (res_a * factor).astype(BF16)
    for j in range(2):
        ob_ref[:, j * BLK:(j + 1) * BLK] = (res_b[j] * factor).astype(BF16)


def local(margin, margin_pattern, orbitals_a, pattern_a, orbitals_b, pattern_b):
    vmem, smem, any_ = (pl.BlockSpec(memory_space=s) for s in (pltpu.VMEM, pltpu.SMEM, pl.ANY))
    dma = pltpu.SemaphoreType.DMA

    def buf(*shape, dtype=BF16):
        return pltpu.VMEM(shape, dtype)

    middle = pl.pallas_call(
        kernel,
        out_shape=(
            jax.ShapeDtypeStruct((2, 16, 32, 256), BF16),
            jax.ShapeDtypeStruct((2, 96, 256), F32),
            jax.ShapeDtypeStruct((2, 96, 256), F32),
        ),
        in_specs=[any_, any_, any_, smem, any_, smem],
        out_specs=(any_, any_, any_),
        scratch_shapes=[
            buf(768, 6144), buf(768, 512), buf(512, 768), buf(32, 384, 128), buf(2, 96, 128), buf(32, 384, 128),
            buf(32, 160, 128), buf(8, 224, 128), buf(24, 224, 128), buf(7, 160, 128),
            buf(768, 256, dtype=F32), buf(2, 4, 96, 256), buf(8, 96, 256),
            buf(16, 32, 256, dtype=F32), buf(16, 32, 256), buf(16, 32, 256),
            buf(8, 32, 256), buf(2, 16, 32, 256), buf(192, 256, dtype=F32), buf(96, 256, dtype=F32),
            buf(2, 96, 256, dtype=F32), buf(2, 96, 256, dtype=F32),
            buf(96, 512), buf(96, 512), pltpu.SMEM((96, 96), jnp.int32),
            dma, dma((3,)), dma, dma((4,)), dma, dma((8,)), dma, dma((2,)), dma, dma((64,)),
            dma, dma((40,)), dma((24,)), dma((4,)), dma, dma((8,)), dma, dma((16,)), dma, dma((8,)),
            dma, dma((16,)), dma, dma, dma, dma, dma((3,)),
        ],
        compiler_params=pltpu.CompilerParams(
            collective_id=0, has_side_effects=True, vmem_limit_bytes=60 << 20
        ),
        name="exchange",
    )(margin, margin_pattern, orbitals_a, pattern_a.T, orbitals_b, pattern_b.T)
    return pl.pallas_call(
        last_kernel,
        out_shape=(
            jax.ShapeDtypeStruct((96, 512), BF16),
            jax.ShapeDtypeStruct((96, 512), BF16),
            jax.ShapeDtypeStruct((512, 512), F32),
        ),
        in_specs=[vmem, vmem, vmem],
        out_specs=(vmem, vmem, vmem),
        compiler_params=pltpu.CompilerParams(vmem_limit_bytes=60 << 20),
        name="last",
    )(*middle)


def solution(mesh):
    in_specs = (P("row", "col"), P(), P(("row", "col"), None), P(), P(("col", "row"), None), P())
    out_specs = (P(("row", "col"), None), P(("col", "row"), None), P())
    return jax.shard_map(local, mesh=mesh, in_specs=in_specs, out_specs=out_specs, check_vma=False)
```

```python
import math

import jax
import jax.numpy as jnp
from jax import lax
from jax.experimental import pallas as pl
from jax.experimental.pallas import tpu as pltpu
from jax.sharding import PartitionSpec as P

MESH = pl.DeviceIdType.MESH
F32 = jnp.float32
BF16 = jnp.bfloat16
BLK = 256
NX, NY, NZ = 4, 4, 8
CH = NX * NZ
PART = ((0, 160), (160, 112), (272, 112))
LATER = range(1, len(PART))
ROWS0, ROWS1 = PART[0][1], max(rows for _, rows in PART[1:])
LEN = ((4, 3), (4, 3), (3, 4), (3, 4), (4, 3))

ORDER = (
    ("z1", 1, 1, 1), ("z1", 1, 0, 1), ("z1", 2, 1, 1), ("z1", 2, 0, 1), ("x0", 1), ("x0", 3), ("apass",),
    ("x1", 1, 0), ("x1", 2, 0), ("x0", 2), ("z1", 1, 1, 2), ("z0", 0, 1, 1), ("x1", 1, 1), ("z1", 1, 0, 2),
    ("z0", 0, 0, 1), ("x1", 1, -1), ("z1", 2, 0, 2), ("z1", 2, 1, 2), ("aturn",), ("terms", 0), ("z0", 3, 1, 1),
    ("z0", 1, 0, 1), ("terms", 1), ("z1", 1, 1, 3), ("z0", 2, 0, 1), ("z0", 1, 1, 1), ("z0", 3, 0, 1), ("x1", 2, 1),
    ("z0", 2, 1, 1), ("z1", 1, 0, 3), ("x1", 1, 2), ("x1", 1, -2), ("terms", 2), ("z1", 2, 1, 3), ("x1", 2, -1),
    ("z0", 0, 1, 2), ("z1", 2, 0, 3), ("x1", 2, -2), ("z0", 3, 1, 2), ("z0", 1, 0, 2), ("z0", 0, 0, 2), ("terms", 3),
    ("u", 1, 4), ("r0", 2, 1, 0), ("z0", 2, 1, 2), ("u", 1, 3), ("x1", 2, 2), ("r0", 3, 1, 0), ("u", 2, 4),
    ("z0", 2, 0, 2), ("r0", 1, 0, 0), ("z0", 3, 0, 2), ("z1", 2, 0, 4), ("u", 2, -3), ("z1", 1, 0, 4), ("x1", 1, -3),
    ("r0", 2, 0, 0), ("r0", 0, 0, 0), ("r0", 0, 1, 0), ("x1", 2, -3), ("bpart", 0), ("z0", 3, 1, 3), ("x1", 1, 3),
    ("r0", 3, 0, 0), ("z0", 1, 1, 2), ("z0", 2, 0, 3), ("x1", 2, 3), ("u", 1, 2), ("z0", 0, 0, 3), ("r0", 2, 1, 1),
    ("r0", 1, 1, 0), ("upass", 1, 4), ("z0", 2, 1, 3), ("r0", 3, 1, 1), ("z0", 1, 0, 3), ("z0", 0, 1, 3), ("u", 2, 2),
    ("upass", 2, 4), ("bpart", 1), ("r0", 0, 1, 1), ("x1", 2, -4), ("x1", 1, -4), ("u", 2, 3), ("r0", 1, 0, 1),
    ("u", 1, -3), ("upass", 1, 2), ("upass", 1, 3), ("z0", 3, 1, 4), ("r0", 0, 0, 1), ("upass", 2, -3),
    ("r0", 2, 0, 1), ("r1", 1, 0, 0), ("u", 2, -2), ("u", 2, -1), ("r0", 3, 0, 1), ("z0", 3, 0, 3), ("z0", 1, 1, 3),
    ("upass", 2, 2), ("u", 1, -1), ("u", 1, 1), ("r0", 2, 1, 2), ("bpart", 2), ("r0", 1, 1, 1), ("r1", 2, 0, 0),
    ("z0", 1, 0, 4), ("z0", 2, 1, 4), ("z0", 0, 0, 4), ("upass", 2, 3), ("bpart", 3), ("r0", 3, 1, 2),
    ("r0", 1, 0, 2), ("orb", 0), ("r0", 0, 1, 2), ("r0", 0, 0, 2), ("r0", 2, 0, 2), ("r0", 2, 1, 3), ("upass", 1, -3),
    ("r1", 1, 0, 1), ("orb", 1), ("r0", 1, 1, 2), ("r0", 3, 1, 3), ("u", 1, -2), ("r0", 3, 0, 2), ("upass", 1, -1),
    ("r0", 1, 0, 3), ("r1", 2, 1, 0), ("upass", 2, -2), ("u", 2, 1), ("r1", 2, 0, 1), ("u", 1, 0), ("upass", 2, -1),
    ("r1", 1, 1, 0), ("u", 2, 0), ("orb2", 0), ("upass", 1, -2), ("r0x", 2), ("orb2", 1), ("r1", 2, 1, 1),
    ("upass", 1, 1), ("r1", 1, 0, 2), ("r1", 2, 0, 2), ("r0x", 1), ("upass", 1, 0), ("upass", 2, 1), ("r0x", 3),
    ("r1", 1, 1, 1), ("upass", 2, 0), ("orb4", 0), ("r0", 0, 0, 3), ("r1", 1, 0, 3), ("orb4", 1), ("r1", 2, 1, 2),
    ("r1", 2, 0, 3), ("r1", 1, 1, 2), ("end0",), ("orbend", 0), ("end1", 2), ("end1", 1), ("orbend", 1),
)


def up(v, n):
    return lax.rem(v, n)


def contract0(a, b):
    return lax.dot_general(a, b, (((0,), (0,)), ((), ())), preferred_element_type=F32)


def split(v):
    high = v.astype(BF16)
    return high, (v - high.astype(F32)).astype(BF16)


def kernel(
    m_ref, pm_hbm, a_hbm, pa_ref, b_hbm, pb_ref,
    r_out, b_out, a_out,
    mbuf, afull, at, bbuf, bst, terms, zbuf, zbuf1, ubuf, xbuf, bacc, bpart, bslots,
    of32, obf, ar1, az, rbuf, aimg, aother, bwhole, awhole, a_ref, b_ref, pm_ref,
    lsem, insem, msend, mrecv, asend, arecv, wsend, wrecv, gsend, grecv,
    rsend, zrecv, urecv, xrecv, bsend, brecv, osend1, orecv1, osend2, orecv2,
    osend4, orecv4, dsend, drecv, ssend, srecv, outsem,
):
    r = lax.axis_index("row")
    y = lax.axis_index("col")
    x, z, c = r // (2 * NZ), (r // 2) % NZ, r % 2
    p = x * NZ + z

    def dev(dx, dz, dy, oc=None):
        core = c if oc is None else oc
        return (up(x + dx, NX) * (2 * NZ) + up(z + dz + NZ, NZ) * 2 + core, up(y + dy, NY))

    def chip(k, dz):
        return up(x + k, NX) * NZ + up(z + dz + NZ, NZ)

    def send(src, dst, ssem, rsem, to):
        pltpu.make_async_remote_copy(
            src_ref=src, dst_ref=dst, send_sem=ssem, recv_sem=rsem, device_id=to, device_id_type=MESH
        ).start()

    def got(dst, sem):
        pltpu.make_async_copy(dst, dst, sem).wait()

    other = 1 - c
    sib = dev(0, 0, 0, other)
    zup, zdown = dev(0, 1, 0), dev(0, -1, 0)

    partners = [sib, zup, zdown] + [dev(k, 0, 0) for k in (1, 2, 3)] + [dev(0, 0, k) for k in (1, 2, 3)]
    bar = pltpu.get_barrier_semaphore()
    for to in partners:
        pl.semaphore_signal(bar, inc=1, device_id=to, device_id_type=MESH)
    loads = []
    for i, (src, dst) in enumerate(((b_hbm, b_ref), (a_hbm, a_ref), (pm_hbm, pm_ref))):
        loads.append(pltpu.make_async_copy(src, dst, insem.at[i]))
        loads[-1].start()
    own_m = mbuf.at[pl.ds(pl.multiple_of(c * 384, 128), 384)]
    local = pltpu.make_async_copy(m_ref, own_m, lsem)
    local.start()

    def masked(ref, pat, d):
        first, last = (96 * d) // BLK, (96 * d + 95) // BLK
        rows = 96 * d + lax.broadcasted_iota(jnp.int32, (96, BLK), 0)
        inside = rows < (first + 1) * BLK
        parts = []
        for k in range(2):
            keep = jnp.where(inside, pat[k, first].astype(F32), pat[k, last].astype(F32))
            parts.append((ref[:, k * BLK:(k + 1) * BLK].astype(F32) * keep).astype(BF16))
        return parts

    loads[0].wait()
    b0, b1 = masked(b_ref, pb_ref, 64 * y + r)
    here = jnp.where(c == 0, b0.astype(F32), b1.astype(F32)).astype(BF16)
    there = jnp.where(c == 0, b1.astype(F32), b0.astype(F32)).astype(BF16)
    brow = pl.multiple_of(96 * c, 16)
    for h in range(2):
        bbuf[p, pl.ds(pl.multiple_of(192 * h + 96 * c, 16), 96), :] = here[:, h * 128:(h + 1) * 128]
        bst[h, :, :] = there[:, h * 128:(h + 1) * 128]

    loads[1].wait()
    arow = pl.multiple_of(384 * c + 96 * y, 16)
    a0, a1 = masked(a_ref, pa_ref, 4 * r + y)
    afull[pl.ds(arow, 96), 0:256] = a0
    afull[pl.ds(arow, 96), 256:512] = a1
    pl.semaphore_wait(bar, len(partners))

    for h in range(2):
        piece = bbuf.at[p, pl.ds(pl.multiple_of(192 * h + 96 * c, 16), 96)]
        send(bst.at[h], piece, wsend, wrecv.at[h], sib)
    def a_rows(core, dy):
        return afull.at[pl.ds(pl.multiple_of(384 * core + 96 * up(y + NY - dy, NY), 16), 96)]

    own_a = a_rows(c, 0)
    send(own_a, own_a, asend, arecv.at[4], sib)
    for dy in (1, 3, 2):
        send(own_a, own_a, asend, arecv.at[dy], dev(0, 0, dy))

    def margin_piece(i):
        def body(t, carry):
            j = 6 * i + t
            cols = pl.ds(pl.multiple_of(BLK * j, BLK), BLK)
            for e in range(3):
                rows = pl.ds(pl.multiple_of(384 * c + 128 * e, 128), 128)
                keep = pm_ref[3 * p + (3 * c + e) // 2, 24 * y + j].astype(F32)
                mbuf[rows, cols] = mbuf[rows, cols] * jnp.full((128, BLK), keep, F32).astype(BF16)
            return carry

        lax.fori_loop(0, 6, body, 0)
        piece = mbuf.at[pl.ds(pl.multiple_of(384 * c, 128), 384), pl.ds(1536 * i, 1536)]
        send(piece, piece, msend, mrecv.at[i], sib)

    local.wait()
    loads[2].wait()
    margin_piece(0)
    margin_piece(1)

    def chunk(h, idx):
        return bbuf.at[idx, pl.ds(*PART[h])]

    def gsend_to(h, idx, to):
        send(chunk(h, idx), chunk(h, idx), gsend, grecv.at[h * CH + idx], to)

    def gwait(h, idx):
        got(chunk(h, idx), grecv.at[h * CH + idx])

    brow2 = pl.multiple_of(96 * other, 16)
    for h in range(2):
        got(bbuf.at[p, pl.ds(pl.multiple_of(192 * h + 96 * other, 16), 96)], wrecv.at[h])
    for h in LATER:
        gsend_to(h, p, zup)
        gsend_to(h, p, zdown)
    for k in (1, 3, 2):
        gsend_to(0, p, dev(k, 0, 0))
    gsend_to(0, p, zup)
    gsend_to(0, p, zdown)
    for h in LATER:
        for k in (1, 3):
            gsend_to(h, p, dev(k, 0, 0))
    margin_piece(2)
    margin_piece(3)

    def do_x0(k):
        gwait(0, chip(k, 0))
        gsend_to(0, chip(k, 0), zup)
        gsend_to(0, chip(k, 0), zdown)

    def do_z0(k, way, s):
        idx = chip(k, s if way else -s)
        gwait(0, idx)
        if s < LEN[k][way]:
            gsend_to(0, idx, zdown if way else zup)

    def do_z1(h, way, s):
        idx = chip(0, s if way else -s)
        gwait(h, idx)
        if s < LEN[4][way]:
            gsend_to(h, idx, zdown if way else zup)
        for k in (1, 3):
            gsend_to(h, idx, dev(k, 0, 0))

    def offsets(s):
        return (0,) if s == 0 else (-s, s) if s < 4 else (-s,)

    def do_x1(h, off):
        odd_chunk = (z + off + NZ) % 2
        gwait(h, chip(1, off))
        gwait(h, chip(3, off))
        gsend_to(h, chip(3 - 2 * odd_chunk, off), dev(1 + 2 * odd_chunk, 0, 0))

    def gather_last(s):
        for off in offsets(s):
            for h in LATER:
                gwait(h, chip(2, off))

    ccol = pl.multiple_of(c * BLK, BLK)

    def term_body(q, carry):
        cols = pl.ds(pl.multiple_of(q * 768, 128), 768)
        both = jnp.dot(at[pl.ds(ccol, BLK), :], mbuf[:, cols], preferred_element_type=F32)
        low_lanes = lax.broadcasted_iota(jnp.int32, (64, 128), 1) < 64
        for u in range(4):
            h, pair = u % 2, u // 2
            whole = both[128 * h:128 * h + 128, 384 * pair:384 * pair + 384]
            top, bottom = whole[0:64, 128:256], whole[64:128, 128:256]
            first = jnp.where(low_lanes, top, pltpu.roll(bottom, 64, 1))
            second = jnp.where(low_lanes, pltpu.roll(top, 64, 1), bottom)
            for e, (tile_e, rest) in enumerate(((whole[:, 0:128], first), (whole[:, 256:384], second))):
                chunk_at = 4 * q + 2 * pair + e
                terms[chunk_at, 192 * h:192 * h + 128, :] = tile_e.astype(BF16)
                terms[chunk_at, 192 * h + 128:192 * h + 192, :] = rest.astype(BF16)
        return carry

    halfz, odd = z // 2, z % 2

    def do_terms(i):
        if i == 0:
            for j in range(4):
                got(mbuf.at[pl.ds(pl.multiple_of(384 * other, 128), 384), pl.ds(1536 * j, 1536)], mrecv.at[j])
        lax.fori_loop(2 * i, 2 * i + 2, term_body, 0)

    def do_bpart(i):
        if i == 0:
            gather_last(0)
        gather_last(i + 1)
        shift = (0, 3 + 2 * odd, 1 + 2 * odd, 2)[i]
        pair = up(halfz + shift, NZ // 2)
        tiles, rows = [], []
        for k in range(NX):
            first = up(x + k, NX) * NZ + 2 * pair
            tiles.append(mbuf[:, pl.ds(pl.multiple_of(192 * first, 128), 384)])
            halves = [bbuf[pl.ds(first, 2), 192 * h:192 * h + 192, :].reshape(384, 128) for h in range(2)]
            rows.append(jnp.concatenate(halves, axis=1))
        part = jnp.dot(
            jnp.concatenate(tiles, axis=1), jnp.concatenate(rows, axis=0), preferred_element_type=F32
        )
        bacc[...] = part if i == 0 else bacc[...] + part

    def do_apass():
        for dy in (1, 3, 2):
            got(a_rows(c, dy), arecv.at[dy])
            send(a_rows(c, dy), a_rows(c, dy), asend, arecv.at[4 + dy], sib)

    def do_aturn():
        for dy in (0, 1, 3, 2):
            got(a_rows(other, dy), arecv.at[4 + dy])
        at[...] = afull[...].T

    def t_at(h, idx):
        return terms.at[idx, pl.ds(*PART[h])]

    def t_val(h, idx):
        return terms[idx, pl.ds(*PART[h]), :].astype(F32)

    order = (4, -3, 3, -2, 2, -1, 1, 0)

    def ways(off):
        odd_chunk = (z + off + NZ) % 2
        return 1 + 2 * odd_chunk, 3 - 2 * odd_chunk

    def uref(h, off, j):
        i = 24 * (h - 1) + 3 * order.index(off) + j
        return ubuf.at[i, pl.ds(0, PART[h][1])], urecv.at[i]

    def usend(src, h, off, j, k):
        dst, sem = uref(h, off, j)
        send(src, dst, rsend, sem, dev(k, 0, 0))

    def do_u(h, off):
        ahead, back = ways(off)
        usend(t_at(h, chip(2, off)), h, off, 0, ahead)
        usend(t_at(h, chip(back, off)), h, off, 1, back)

    def do_upass(h, off):
        ahead, _ = ways(off)
        ref, sem = uref(h, off, 0)
        got(ref, sem)
        ref[...] = (ref[...].astype(F32) + t_val(h, chip(ahead, off))).astype(BF16)
        usend(ref, h, off, 2, ahead)

    def usum(h, off):
        total = t_val(h, chip(0, off))
        for j in (1, 2):
            ref, sem = uref(h, off, j)
            got(ref, sem)
            total += ref[...].astype(F32)
        return total

    def zref(h, k, way, s):
        if h:
            slot = 8 * (h - 1) + 4 * way + s
            return zbuf1.at[slot, pl.ds(0, PART[h][1])], zrecv.at[32 + slot]
        slot = 8 * k + 4 * way + s
        return zbuf.at[slot], zrecv.at[slot]

    def zsend(src, h, k, way, s):
        dst, sem = zref(h, k, way, s)
        send(src, dst, rsend, sem, zup if way == 0 else zdown)

    def do_r0(k, way, s):
        lim = LEN[k][way]
        idx = chip(k, (s - lim) if way else (lim - s))
        if s == 0:
            zsend(t_at(0, idx), 0, k, way, 0)
        else:
            ref, sem = zref(0, k, way, s - 1)
            got(ref, sem)
            ref[...] = (ref[...].astype(F32) + t_val(0, idx)).astype(BF16)
            zsend(ref, 0, k, way, s)

    def do_r1(h, way, s):
        lim = LEN[4][way]
        off = (s - lim) if way else (lim - s)
        total = usum(h, off)
        if s > 0:
            ref, sem = zref(h, 4, way, s - 1)
            got(ref, sem)
            total += ref[...].astype(F32)
        mine = uref(h, off, 1)[0]
        mine[...] = total.astype(BF16)
        zsend(mine, h, 4, way, s)

    def plane():
        return [(4 * dx + dy, dx, dy) for dx in range(NX) for dy in range(NY) if dx or dy]

    def strip(a):
        return pl.ds(16 * a, 16)

    def do_orb(a):
        if a == 0:
            b_all = bacc[...]
            high = b_all.astype(BF16)
            low = (b_all - high.astype(F32)).astype(BF16)
            bpart[...] = high.reshape(2, NY, 96, BLK)
            orb = jnp.dot(at[...], high, preferred_element_type=F32)
            orb += jnp.dot(at[...], low, preferred_element_type=F32)
            orb = orb.reshape(16, 32, BLK)
            of32[...] = orb
            obf[...] = orb.astype(BF16)
        for slot, dx, dy in plane():
            src = obf.at[up(x + dx, NX) * 4 + up(y + dy, NY), strip(a)]
            send(src, ar1.at[slot, strip(a)], osend1, orecv1.at[16 * a + slot], dev(dx, 0, dy))
        if a == 1:
            for dy in range(NY):
                for oc in range(2):
                    if dy or oc:
                        core = c if oc == 0 else other
                        slot = 2 * dy + oc
                        src = bpart.at[core, up(y + dy, NY)]
                        send(src, bslots.at[slot], bsend, brecv.at[slot], dev(0, 0, dy, core))
            bslots[0] = bpart[c, y]

    def do_orb2(a):
        total = of32[4 * x + y, strip(a), :]
        for slot, _, _ in plane():
            got(ar1.at[slot, strip(a)], orecv1.at[16 * a + slot])
            total += ar1[slot, strip(a), :].astype(F32)
        mine = az.at[z, strip(a)]
        mine[...] = total.astype(BF16)
        for dz in (4, 3, 5, 2, 6, 1, 7):
            send(mine, mine, osend2, orecv2.at[8 * a + dz], dev(0, dz, 0))

    def do_orb4(a):
        for dz in range(1, NZ):
            got(az.at[up(z - dz + NZ, NZ), strip(a)], orecv2.at[8 * a + dz])
        total = az[0, strip(a), :].astype(F32)
        for i in range(1, NZ):
            total += az[i, strip(a), :].astype(F32)
        mine = rbuf.at[c, 4 * x + y, strip(a)]
        mine[...] = (total * (1.0 / math.sqrt(24576))).astype(BF16)
        for slot, dx, dy in plane():
            send(mine, mine, osend4, orecv4.at[16 * a + slot], dev(dx, 0, dy))

    def zlast(h, k):
        total = usum(h, 0) if h else t_val(0, chip(k, 0))
        for way in range(2):
            ref, sem = zref(h, k, way, LEN[k][way] - 1)
            got(ref, sem)
            total += ref[...].astype(F32)
        return total

    def do_r0x(k):
        xbuf[k] = zlast(0, k).astype(BF16)
        send(xbuf.at[k], xbuf.at[3 + k], rsend, xrecv.at[k], dev(k, 0, 0))

    pieces = {}

    def do_end0():
        total = zlast(0, 0)
        for k in (1, 3, 2):
            got(xbuf.at[3 + k], xrecv.at[k])
            total += xbuf[3 + k].astype(F32)
        pieces[0] = total
        for oc in range(2):
            total = 0.0
            for dy in range(NY):
                slot = 2 * dy + oc
                if slot:
                    got(bslots.at[slot], brecv.at[slot])
                total += bslots[slot].astype(F32)
            bwhole[c if oc == 0 else other] = total
        pltpu.make_async_copy(bwhole, b_out, outsem.at[0]).start()

    def do_end1(h):
        pieces[h] = zlast(h, 4)

    def do_orbend(a):
        for slot, dx, dy in plane():
            src = up(x - dx + NX, NX) * 4 + up(y - dy + NY, NY)
            got(rbuf.at[c, src, strip(a)], orecv4.at[16 * a + slot])
        half = rbuf.at[c, pl.ds(0, 16), strip(a)]
        send(half, half, dsend, drecv.at[a], sib)

    steps = dict(
        x0=do_x0, z0=do_z0, z1=do_z1, x1=do_x1, apass=do_apass, aturn=do_aturn, terms=do_terms, bpart=do_bpart,
        u=do_u, upass=do_upass, r0=do_r0, r1=do_r1, r0x=do_r0x, orb=do_orb, orb2=do_orb2, orb4=do_orb4,
        orbend=do_orbend, end0=do_end0, end1=do_end1,
    )
    for name, *where in ORDER:
        steps[name](*where)

    image = jnp.concatenate([pieces[h] for h in range(len(PART))], axis=0)
    for h in range(2):
        lanes = pl.ds(128 * h, 128)
        packed = image[192 * h + 128:192 * h + 192, :]
        rest = jnp.concatenate([packed, pltpu.roll(packed, 64, 1)], axis=0).T
        aimg[pl.ds(pl.multiple_of(64 * odd, 8), 128), lanes] = image[192 * h:192 * h + 128, :].T
        aimg[pl.ds(pl.multiple_of(128 * (1 - odd), 8), 64), lanes] = rest[0:64, :]
    send(aimg.at[pl.ds(pl.multiple_of(96 * other, 8), 96)], aother, ssend, srecv, sib)
    for a in range(2):
        got(rbuf.at[other, pl.ds(0, 16), strip(a)], drecv.at[a])
    pltpu.make_async_copy(rbuf, r_out, outsem.at[1]).start()
    awhole[c] = aimg[pl.ds(brow, 96), :]
    got(aother, srecv)
    awhole[other] = aother[...]
    pltpu.make_async_copy(awhole, a_out, outsem.at[2]).start()

    for i, (src, dst) in enumerate(((bwhole, b_out), (rbuf, r_out), (awhole, a_out))):
        pltpu.make_async_copy(src, dst, outsem.at[i]).wait()
    got(bst, wsend)
    got(afull.at[pl.ds(0, 672)], asend)
    got(own_m, msend)
    got(bbuf.at[pl.ds(0, 31)], gsend)
    got(bbuf.at[pl.ds(0, 31)], rsend)
    got(bslots.at[pl.ds(1, 7)], bsend)
    got(obf.at[pl.ds(0, 15)], osend1)
    got(obf.at[pl.ds(0, 7)], osend2)
    got(obf.at[pl.ds(0, 15)], osend4)
    got(rbuf.at[c], dsend)
    got(aother, ssend)


def last_kernel(r_ref, b_ref, a_ref, oa_ref, ob_ref, oo_ref):
    factor = 1.0 / math.sqrt(512)
    res_a, res_b = 0.0, [0.0, 0.0]
    for h in range(2):
        oo_ref[:, h * BLK:(h + 1) * BLK] = r_ref[h].reshape(512, BLK).astype(F32)
    for h in range(2):
        half = r_ref[h].reshape(512, BLK)
        for v in split(b_ref[h]):
            res_a += lax.dot_general(v, half, (((1,), (1,)), ((), ())), preferred_element_type=F32)
        for v in split(a_ref[h]):
            for j in range(2):
                rows = r_ref[j, 8 * h:8 * h + 8].reshape(BLK, BLK)
                res_b[j] += jnp.dot(v, rows, preferred_element_type=F32)
    oa_ref[...] = (res_a * factor).astype(BF16)
    for j in range(2):
        ob_ref[:, j * BLK:(j + 1) * BLK] = (res_b[j] * factor).astype(BF16)


def local(margin, margin_pattern, orbitals_a, pattern_a, orbitals_b, pattern_b):
    vmem, smem, any_ = (pl.BlockSpec(memory_space=s) for s in (pltpu.VMEM, pltpu.SMEM, pl.ANY))
    dma = pltpu.SemaphoreType.DMA
    later = len(LATER)

    def buf(*shape, dtype=BF16):
        return pltpu.VMEM(shape, dtype)

    middle = pl.pallas_call(
        kernel,
        out_shape=(
            jax.ShapeDtypeStruct((2, 16, 32, 256), BF16),
            jax.ShapeDtypeStruct((2, 96, 256), F32),
            jax.ShapeDtypeStruct((2, 96, 256), F32),
        ),
        in_specs=[any_, any_, any_, smem, any_, smem],
        out_specs=(any_, any_, any_),
        scratch_shapes=[
            buf(768, 6144), buf(768, 512), buf(512, 768), buf(32, 384, 128), buf(2, 96, 128), buf(32, 384, 128),
            buf(32, ROWS0, 128), buf(8 * later, ROWS1, 128), buf(24 * later, ROWS1, 128), buf(7, ROWS0, 128),
            buf(768, 256, dtype=F32), buf(2, 4, 96, 256), buf(8, 96, 256),
            buf(16, 32, 256, dtype=F32), buf(16, 32, 256), buf(16, 32, 256),
            buf(8, 32, 256), buf(2, 16, 32, 256), buf(192, 256, dtype=F32), buf(96, 256, dtype=F32),
            buf(2, 96, 256, dtype=F32), buf(2, 96, 256, dtype=F32),
            buf(96, 512), buf(96, 512), pltpu.SMEM((96, 96), jnp.int32),
            dma, dma((3,)), dma, dma((4,)), dma, dma((8,)), dma, dma((2,)), dma, dma((CH * len(PART),)),
            dma, dma((32 + 8 * later,)), dma((24 * later,)), dma((4,)), dma, dma((8,)), dma, dma((32,)), dma, dma((16,)),
            dma, dma((32,)), dma, dma((2,)), dma, dma, dma((3,)),
        ],
        compiler_params=pltpu.CompilerParams(
            collective_id=0, has_side_effects=True, vmem_limit_bytes=60 << 20
        ),
        name="exchange",
    )(margin, margin_pattern, orbitals_a, pattern_a.T, orbitals_b, pattern_b.T)
    return pl.pallas_call(
        last_kernel,
        out_shape=(
            jax.ShapeDtypeStruct((96, 512), BF16),
            jax.ShapeDtypeStruct((96, 512), BF16),
            jax.ShapeDtypeStruct((512, 512), F32),
        ),
        in_specs=[vmem, vmem, vmem],
        out_specs=(vmem, vmem, vmem),
        compiler_params=pltpu.CompilerParams(vmem_limit_bytes=60 << 20),
        name="last",
    )(*middle)


def solution(mesh):
    in_specs = (P("row", "col"), P(), P(("row", "col"), None), P(), P(("col", "row"), None), P())
    out_specs = (P(("row", "col"), None), P(("col", "row"), None), P())
    return jax.shard_map(local, mesh=mesh, in_specs=in_specs, out_specs=out_specs, check_vma=False)
```

```python
import math

import jax
import jax.numpy as jnp
from jax import lax
from jax.experimental import pallas as pl
from jax.experimental.pallas import tpu as pltpu
from jax.sharding import PartitionSpec as P

MESH = pl.DeviceIdType.MESH
F32 = jnp.float32
BF16 = jnp.bfloat16
BLK = 256
NX, NY, NZ = 4, 4, 8
CH = NX * NZ
PART = ((0, 160), (160, 128), (288, 96))
USED = tuple(start // 2 for start, _ in PART)
LATER = range(1, len(PART))
ROWS0, ROWS1 = PART[0][1], max(rows for _, rows in PART[1:])
LEN = ((4, 3), (4, 3), (3, 4), (3, 4), (4, 3))

ORDER = (
    ("z1", 1, 0, 1), ("z1", 1, 1, 1), ("x0", 3), ("z1", 2, 1, 1), ("z1", 2, 0, 1), ("z0", 0, 0, 1), ("z0", 0, 1, 1),
    ("z1", 1, 0, 2), ("apass",), ("z1", 1, 1, 2), ("x1", 1, 0), ("x0", 1), ("x1", 1, -1), ("x1", 1, 1),
    ("z1", 2, 0, 2), ("x1", 2, 1), ("z0", 3, 0, 1), ("z0", 3, 1, 1), ("z1", 2, 1, 2), ("x0", 2), ("x1", 2, 0),
    ("aturn",), ("terms", 0), ("x1", 1, -2), ("z1", 1, 1, 3), ("z0", 0, 0, 2), ("z1", 1, 0, 3), ("terms", 1),
    ("z1", 2, 0, 3), ("z0", 1, 0, 1), ("x1", 2, -1), ("z0", 1, 1, 1), ("terms", 2), ("z0", 3, 1, 2), ("x1", 1, 2),
    ("z0", 0, 1, 2), ("z1", 2, 1, 3), ("z0", 2, 0, 1), ("z0", 3, 0, 2), ("terms", 3), ("u", 1, 4), ("z0", 2, 1, 1),
    ("r0", 2, 1, 0), ("u", 2, 4), ("r0", 0, 0, 0), ("r0", 3, 1, 0), ("r0", 1, 0, 0), ("x1", 2, 2), ("z1", 2, 0, 4),
    ("x1", 1, 3), ("u", 2, -3), ("z1", 1, 0, 4), ("x1", 2, -2), ("z0", 3, 1, 3), ("x1", 2, -3), ("z0", 1, 0, 2),
    ("x1", 1, -3), ("z0", 2, 1, 2), ("z0", 0, 0, 3), ("r0", 3, 0, 0), ("upass", 2, 4), ("upass", 1, 4),
    ("r0", 2, 1, 1), ("x1", 2, 3), ("u", 1, -3), ("x1", 2, -4), ("u", 1, 3), ("z0", 1, 1, 2), ("z0", 2, 0, 2),
    ("bpart", 0), ("u", 2, 3), ("r0", 1, 1, 0), ("z0", 1, 0, 3), ("r0", 2, 0, 0), ("x1", 1, -4), ("u", 1, -2),
    ("z0", 3, 1, 4), ("z0", 0, 1, 3), ("z0", 0, 0, 4), ("r0", 1, 0, 1), ("u", 2, -1), ("z0", 3, 0, 3),
    ("z0", 2, 1, 3), ("r0", 3, 1, 1), ("r0", 0, 0, 1), ("upass", 2, -3), ("bpart", 1), ("r0", 3, 0, 1),
    ("upass", 1, -3), ("r0", 0, 1, 0), ("z0", 2, 0, 3), ("u", 1, 2), ("u", 2, -2), ("u", 1, -1), ("r0", 2, 1, 2),
    ("r1", 2, 0, 0), ("upass", 1, 3), ("z0", 1, 1, 3), ("u", 2, 2), ("z0", 1, 0, 4), ("r0", 1, 1, 1), ("r1", 1, 0, 0),
    ("upass", 2, 3), ("bpart", 2), ("z0", 2, 1, 4), ("r0", 2, 0, 1), ("bpart", 3), ("r0", 1, 0, 2), ("r0", 3, 1, 2),
    ("upass", 1, -2), ("orb", 0), ("orb", 1), ("r0", 3, 0, 2), ("r0", 2, 1, 3), ("u", 2, 1), ("r0", 1, 1, 2),
    ("r0", 0, 0, 2), ("r1", 1, 0, 1), ("r1", 2, 1, 0), ("u", 2, 0), ("upass", 2, -2), ("upass", 1, 2),
    ("upass", 2, 2), ("u", 1, 0), ("u", 1, 1), ("r1", 1, 1, 0), ("r0", 2, 0, 2), ("r0", 0, 1, 1), ("r0", 1, 0, 3),
    ("r0", 3, 1, 3), ("r1", 2, 0, 1), ("orb2", 0), ("upass", 1, -1), ("orb2", 1), ("r0x", 2), ("r1", 2, 1, 1),
    ("r0x", 1), ("upass", 2, 1), ("upass", 2, -1), ("upass", 2, 0), ("upass", 1, 1), ("r1", 2, 0, 2), ("r1", 1, 1, 1),
    ("r1", 1, 0, 2), ("r0", 0, 0, 3), ("upass", 1, 0), ("r0", 0, 1, 2), ("r0x", 3), ("orb4", 0), ("r1", 2, 1, 2),
    ("orb4", 1), ("r1", 2, 0, 3), ("r1", 1, 0, 3), ("r1", 1, 1, 2), ("end0",), ("orbend", 0), ("end1", 2),
    ("end1", 1), ("orbend", 1),
)


def up(v, n):
    return lax.rem(v, n)


def spots(core, block):
    found = []
    for (start, rows), used in zip(PART, USED):
        low, high = max(used, 96 * block), min(used + rows // 2, 96 * block + 96)
        if low < high:
            found.append((start + core * rows // 2 + low - used, high - low))
    return found


def contract0(a, b):
    return lax.dot_general(a, b, (((0,), (0,)), ((), ())), preferred_element_type=F32)


def split(v):
    high = v.astype(BF16)
    return high, (v - high.astype(F32)).astype(BF16)


def kernel(
    m_ref, pm_hbm, a_hbm, pa_ref, b_hbm, pb_ref,
    r_out, b_out, a_out,
    mbuf, afull, at, bbuf, bst, terms, zbuf, zbuf1, ubuf, xbuf, bacc, bpart, bslots,
    of32, obf, ar1, az, rbuf, aimg, aother, bwhole, a_ref, b_ref, pm_ref,
    lsem, insem, msend, mrecv, asend, arecv, wsend, wrecv, gsend, grecv,
    rsend, zrecv, urecv, xrecv, bsend, brecv, osend1, orecv1, osend2, orecv2,
    osend4, orecv4, dsend, drecv, ssend, srecv, outsem,
):
    r = lax.axis_index("row")
    y = lax.axis_index("col")
    x, z, c = r // (2 * NZ), (r // 2) % NZ, r % 2
    p = x * NZ + z

    def dev(dx, dz, dy, oc=None):
        core = c if oc is None else oc
        return (up(x + dx, NX) * (2 * NZ) + up(z + dz + NZ, NZ) * 2 + core, up(y + dy, NY))

    def chip(k, dz):
        return up(x + k, NX) * NZ + up(z + dz + NZ, NZ)

    def send(src, dst, ssem, rsem, to):
        pltpu.make_async_remote_copy(
            src_ref=src, dst_ref=dst, send_sem=ssem, recv_sem=rsem, device_id=to, device_id_type=MESH
        ).start()

    def got(dst, sem):
        pltpu.make_async_copy(dst, dst, sem).wait()

    other = 1 - c
    sib = dev(0, 0, 0, other)
    zup, zdown = dev(0, 1, 0), dev(0, -1, 0)

    partners = [sib] + [dev(0, 0, k) for k in (1, 2, 3)]
    for core in (c, other):
        partners += [dev(0, 1, 0, core), dev(0, -1, 0, core)] + [dev(k, 0, 0, core) for k in (1, 2, 3)]
    bar = pltpu.get_barrier_semaphore()
    for to in partners:
        pl.semaphore_signal(bar, inc=1, device_id=to, device_id_type=MESH)
    loads = []
    for i, (src, dst) in enumerate(((b_hbm, b_ref), (a_hbm, a_ref), (pm_hbm, pm_ref))):
        loads.append(pltpu.make_async_copy(src, dst, insem.at[i]))
        loads[-1].start()
    own_m = mbuf.at[pl.ds(pl.multiple_of(c * 384, 128), 384)]
    local = pltpu.make_async_copy(m_ref, own_m, lsem)
    local.start()

    def masked(ref, pat, d):
        first, last = (96 * d) // BLK, (96 * d + 95) // BLK
        rows = 96 * d + lax.broadcasted_iota(jnp.int32, (96, BLK), 0)
        inside = rows < (first + 1) * BLK
        parts = []
        for k in range(2):
            keep = jnp.where(inside, pat[k, first].astype(F32), pat[k, last].astype(F32))
            parts.append((ref[:, k * BLK:(k + 1) * BLK].astype(F32) * keep).astype(BF16))
        return parts

    loads[0].wait()
    b0, b1 = masked(b_ref, pb_ref, 64 * y + r)
    here = jnp.where(c == 0, b0.astype(F32), b1.astype(F32)).astype(BF16)
    there = jnp.where(c == 0, b1.astype(F32), b0.astype(F32)).astype(BF16)
    brow = pl.multiple_of(96 * c, 16)
    here = jnp.concatenate([here[:, 0:128], here[:, 128:256]], axis=0)
    bst[...] = jnp.concatenate([there[:, 0:128], there[:, 128:256]], axis=0)

    def own_piece(h):
        start, rows = PART[h]
        return bbuf.at[p, pl.ds(pl.multiple_of(start + c * (rows // 2), 16), rows // 2)]

    def other_piece(h):
        return bst.at[pl.ds(USED[h], PART[h][1] // 2)]

    for h in range(len(PART)):
        own_piece(h)[...] = here[USED[h]:USED[h] + PART[h][1] // 2, :]
    loads[1].wait()
    arow = pl.multiple_of(384 * c + 96 * y, 16)
    a0, a1 = masked(a_ref, pa_ref, 4 * r + y)
    afull[pl.ds(arow, 96), 0:256] = a0
    afull[pl.ds(arow, 96), 256:512] = a1
    pl.semaphore_wait(bar, len(partners))

    def chunk(h, idx):
        return bbuf.at[idx, pl.ds(*PART[h])]

    def gsend_to(h, idx, to):
        send(chunk(h, idx), chunk(h, idx), gsend, grecv.at[h * CH + idx], to)

    def gwait(h, idx):
        got(chunk(h, idx), grecv.at[h * CH + idx])

    def first_send(h, dx, dz):
        send(own_piece(h), own_piece(h), gsend, grecv.at[h * CH + p], dev(dx, dz, 0))
        send(other_piece(h), own_piece(h), gsend, grecv.at[h * CH + p], dev(dx, dz, 0, other))

    for h in LATER:
        first_send(h, 0, 1)
        first_send(h, 0, -1)
    for k in (1, 3, 2):
        first_send(0, k, 0)
    first_send(0, 0, 1)
    first_send(0, 0, -1)
    for h in LATER:
        for k in (1, 3):
            first_send(h, k, 0)
    for h in range(len(PART)):
        send(other_piece(h), own_piece(h), wsend, wrecv, sib)

    def a_rows(core, dy):
        return afull.at[pl.ds(pl.multiple_of(384 * core + 96 * up(y + NY - dy, NY), 16), 96)]

    own_a = a_rows(c, 0)
    send(own_a, own_a, asend, arecv.at[4], sib)
    for dy in (1, 3, 2):
        send(own_a, own_a, asend, arecv.at[dy], dev(0, 0, dy))

    def margin_piece(i):
        def body(t, carry):
            j = 6 * i + t
            cols = pl.ds(pl.multiple_of(BLK * j, BLK), BLK)
            for e in range(3):
                rows = pl.ds(pl.multiple_of(384 * c + 128 * e, 128), 128)
                keep = pm_ref[3 * p + (3 * c + e) // 2, 24 * y + j].astype(F32)
                mbuf[rows, cols] = mbuf[rows, cols] * jnp.full((128, BLK), keep, F32).astype(BF16)
            return carry

        lax.fori_loop(0, 6, body, 0)
        piece = mbuf.at[pl.ds(pl.multiple_of(384 * c, 128), 384), pl.ds(1536 * i, 1536)]
        send(piece, piece, msend, mrecv.at[i], sib)

    local.wait()
    loads[2].wait()
    margin_piece(0)
    margin_piece(1)

    margin_piece(2)
    margin_piece(3)

    def do_x0(k):
        gwait(0, chip(k, 0))
        gsend_to(0, chip(k, 0), zup)
        gsend_to(0, chip(k, 0), zdown)

    def do_z0(k, way, s):
        idx = chip(k, s if way else -s)
        gwait(0, idx)
        if s < LEN[k][way]:
            gsend_to(0, idx, zdown if way else zup)

    def do_z1(h, way, s):
        idx = chip(0, s if way else -s)
        gwait(h, idx)
        if s < LEN[4][way]:
            gsend_to(h, idx, zdown if way else zup)
        for k in (1, 3):
            gsend_to(h, idx, dev(k, 0, 0))

    def offsets(s):
        return (0,) if s == 0 else (-s, s) if s < 4 else (-s,)

    def do_x1(h, off):
        odd_chunk = (z + off + NZ) % 2
        gwait(h, chip(1, off))
        gwait(h, chip(3, off))
        gsend_to(h, chip(3 - 2 * odd_chunk, off), dev(1 + 2 * odd_chunk, 0, 0))

    def gather_last(s):
        for off in offsets(s):
            for h in LATER:
                gwait(h, chip(2, off))

    ccol = pl.multiple_of(c * BLK, BLK)

    def term_body(q, carry):
        cols = pl.ds(pl.multiple_of(q * 768, 128), 768)
        both = jnp.dot(at[pl.ds(ccol, BLK), :], mbuf[:, cols], preferred_element_type=F32)
        low_lanes = lax.broadcasted_iota(jnp.int32, (64, 128), 1) < 64
        for u in range(4):
            h, pair = u % 2, u // 2
            whole = both[128 * h:128 * h + 128, 384 * pair:384 * pair + 384]
            top, bottom = whole[0:64, 128:256], whole[64:128, 128:256]
            first = jnp.where(low_lanes, top, pltpu.roll(bottom, 64, 1))
            second = jnp.where(low_lanes, pltpu.roll(top, 64, 1), bottom)
            for e, (tile_e, rest) in enumerate(((whole[:, 0:128], first), (whole[:, 256:384], second))):
                chunk_at = 4 * q + 2 * pair + e
                terms[chunk_at, 192 * h:192 * h + 128, :] = tile_e.astype(BF16)
                terms[chunk_at, 192 * h + 128:192 * h + 192, :] = rest.astype(BF16)
        return carry

    halfz, odd = z // 2, z % 2

    def do_terms(i):
        if i == 0:
            for j in range(4):
                got(mbuf.at[pl.ds(pl.multiple_of(384 * other, 128), 384), pl.ds(1536 * j, 1536)], mrecv.at[j])
        lax.fori_loop(2 * i, 2 * i + 2, term_body, 0)

    def do_bpart(i):
        if i == 0:
            got(bst, wrecv)
            gather_last(0)
        gather_last(i + 1)
        shift = (0, 3 + 2 * odd, 1 + 2 * odd, 2)[i]
        pair = up(halfz + shift, NZ // 2)
        tiles, rows = [], []
        for k in range(NX):
            first = up(x + k, NX) * NZ + 2 * pair
            tiles.append(mbuf[:, pl.ds(pl.multiple_of(192 * first, 128), 384)])
            halves = []
            for block in range(2):
                found = [(e, spot) for e in range(2) for core in range(2) for spot in spots(core, block)]
                halves.append(jnp.concatenate([bbuf[first + e, a:a + n, :] for e, (a, n) in found], axis=0))
            rows.append(jnp.concatenate(halves, axis=1))
        part = jnp.dot(
            jnp.concatenate(tiles, axis=1), jnp.concatenate(rows, axis=0), preferred_element_type=F32
        )
        bacc[...] = part if i == 0 else bacc[...] + part

    def do_apass():
        for dy in (1, 3, 2):
            got(a_rows(c, dy), arecv.at[dy])
            send(a_rows(c, dy), a_rows(c, dy), asend, arecv.at[4 + dy], sib)

    def do_aturn():
        for dy in (0, 1, 3, 2):
            got(a_rows(other, dy), arecv.at[4 + dy])
        at[...] = afull[...].T

    def t_at(h, idx):
        return terms.at[idx, pl.ds(*PART[h])]

    def t_val(h, idx):
        return terms[idx, pl.ds(*PART[h]), :].astype(F32)

    order = (4, -3, 3, -2, 2, -1, 1, 0)

    def ways(off):
        odd_chunk = (z + off + NZ) % 2
        return 1 + 2 * odd_chunk, 3 - 2 * odd_chunk

    def uref(h, off, j):
        i = 24 * (h - 1) + 3 * order.index(off) + j
        return ubuf.at[i, pl.ds(0, PART[h][1])], urecv.at[i]

    def usend(src, h, off, j, k):
        dst, sem = uref(h, off, j)
        send(src, dst, rsend, sem, dev(k, 0, 0))

    def do_u(h, off):
        ahead, back = ways(off)
        usend(t_at(h, chip(2, off)), h, off, 0, ahead)
        usend(t_at(h, chip(back, off)), h, off, 1, back)

    def do_upass(h, off):
        ahead, _ = ways(off)
        ref, sem = uref(h, off, 0)
        got(ref, sem)
        ref[...] = (ref[...].astype(F32) + t_val(h, chip(ahead, off))).astype(BF16)
        usend(ref, h, off, 2, ahead)

    def usum(h, off):
        total = t_val(h, chip(0, off))
        for j in (1, 2):
            ref, sem = uref(h, off, j)
            got(ref, sem)
            total += ref[...].astype(F32)
        return total

    def zref(h, k, way, s):
        if h:
            slot = 8 * (h - 1) + 4 * way + s
            return zbuf1.at[slot, pl.ds(0, PART[h][1])], zrecv.at[32 + slot]
        slot = 8 * k + 4 * way + s
        return zbuf.at[slot], zrecv.at[slot]

    def zsend(src, h, k, way, s):
        dst, sem = zref(h, k, way, s)
        send(src, dst, rsend, sem, zup if way == 0 else zdown)

    def do_r0(k, way, s):
        lim = LEN[k][way]
        idx = chip(k, (s - lim) if way else (lim - s))
        if s == 0:
            zsend(t_at(0, idx), 0, k, way, 0)
        else:
            ref, sem = zref(0, k, way, s - 1)
            got(ref, sem)
            ref[...] = (ref[...].astype(F32) + t_val(0, idx)).astype(BF16)
            zsend(ref, 0, k, way, s)

    def do_r1(h, way, s):
        lim = LEN[4][way]
        off = (s - lim) if way else (lim - s)
        total = usum(h, off)
        if s > 0:
            ref, sem = zref(h, 4, way, s - 1)
            got(ref, sem)
            total += ref[...].astype(F32)
        mine = uref(h, off, 1)[0]
        mine[...] = total.astype(BF16)
        zsend(mine, h, 4, way, s)

    def plane():
        return [(4 * dx + dy, dx, dy) for dx in range(NX) for dy in range(NY) if dx or dy]

    def strip(a):
        return pl.ds(16 * a, 16)

    def do_orb(a):
        if a == 0:
            b_all = bacc[...]
            high = b_all.astype(BF16)
            low = (b_all - high.astype(F32)).astype(BF16)
            bpart[...] = high.reshape(2, NY, 96, BLK)
            orb = jnp.dot(at[...], high, preferred_element_type=F32)
            orb += jnp.dot(at[...], low, preferred_element_type=F32)
            orb = orb.reshape(16, 32, BLK)
            of32[...] = orb
            obf[...] = orb.astype(BF16)
        for slot, dx, dy in plane():
            src = obf.at[up(x + dx, NX) * 4 + up(y + dy, NY), strip(a)]
            send(src, ar1.at[slot, strip(a)], osend1, orecv1.at[16 * a + slot], dev(dx, 0, dy))
        if a == 1:
            for dy in range(NY):
                for oc in range(2):
                    if dy or oc:
                        core = c if oc == 0 else other
                        slot = 2 * dy + oc
                        src = bpart.at[core, up(y + dy, NY)]
                        send(src, bslots.at[slot], bsend, brecv.at[slot], dev(0, 0, dy, core))
            bslots[0] = bpart[c, y]

    def do_orb2(a):
        total = of32[4 * x + y, strip(a), :]
        for slot, _, _ in plane():
            got(ar1.at[slot, strip(a)], orecv1.at[16 * a + slot])
            total += ar1[slot, strip(a), :].astype(F32)
        mine = az.at[z, strip(a)]
        mine[...] = total.astype(BF16)
        for dz in (4, 3, 5, 2, 6, 1, 7):
            send(mine, mine, osend2, orecv2.at[8 * a + dz], dev(0, dz, 0))

    def do_orb4(a):
        for dz in range(1, NZ):
            got(az.at[up(z - dz + NZ, NZ), strip(a)], orecv2.at[8 * a + dz])
        total = az[0, strip(a), :].astype(F32)
        for i in range(1, NZ):
            total += az[i, strip(a), :].astype(F32)
        mine = rbuf.at[c, 4 * x + y, strip(a)]
        mine[...] = (total * (1.0 / math.sqrt(24576))).astype(BF16)
        for slot, dx, dy in plane():
            send(mine, mine, osend4, orecv4.at[16 * a + slot], dev(dx, 0, dy))

    def zlast(h, k):
        total = usum(h, 0) if h else t_val(0, chip(k, 0))
        for way in range(2):
            ref, sem = zref(h, k, way, LEN[k][way] - 1)
            got(ref, sem)
            total += ref[...].astype(F32)
        return total

    def do_r0x(k):
        xbuf[k] = zlast(0, k).astype(BF16)
        send(xbuf.at[k], xbuf.at[3 + k], rsend, xrecv.at[k], dev(k, 0, 0))

    pieces = {}

    def do_end0():
        total = zlast(0, 0)
        for k in (1, 3, 2):
            got(xbuf.at[3 + k], xrecv.at[k])
            total += xbuf[3 + k].astype(F32)
        pieces[0] = total
        for oc in range(2):
            total = 0.0
            for dy in range(NY):
                slot = 2 * dy + oc
                if slot:
                    got(bslots.at[slot], brecv.at[slot])
                total += bslots[slot].astype(F32)
            bwhole[c if oc == 0 else other] = total
        pltpu.make_async_copy(bwhole, b_out, outsem.at[0]).start()

    def do_end1(h):
        pieces[h] = zlast(h, 4)

    def do_orbend(a):
        for slot, dx, dy in plane():
            src = up(x - dx + NX, NX) * 4 + up(y - dy + NY, NY)
            got(rbuf.at[c, src, strip(a)], orecv4.at[16 * a + slot])
        half = rbuf.at[c, pl.ds(0, 16), strip(a)]
        send(half, half, dsend, drecv.at[a], sib)

    steps = dict(
        x0=do_x0, z0=do_z0, z1=do_z1, x1=do_x1, apass=do_apass, aturn=do_aturn, terms=do_terms, bpart=do_bpart,
        u=do_u, upass=do_upass, r0=do_r0, r1=do_r1, r0x=do_r0x, orb=do_orb, orb2=do_orb2, orb4=do_orb4,
        orbend=do_orbend, end0=do_end0, end1=do_end1,
    )
    for name, *where in ORDER:
        steps[name](*where)

    image = jnp.concatenate([pieces[h] for h in range(len(PART))], axis=0)
    for h in range(2):
        lanes = pl.ds(128 * h, 128)
        packed = image[192 * h + 128:192 * h + 192, :]
        rest = jnp.concatenate([packed, pltpu.roll(packed, 64, 1)], axis=0).T
        aimg[pl.ds(pl.multiple_of(64 * odd, 8), 128), lanes] = image[192 * h:192 * h + 128, :].T
        aimg[pl.ds(pl.multiple_of(128 * (1 - odd), 8), 64), lanes] = rest[0:64, :]
    send(aimg.at[pl.ds(pl.multiple_of(96 * other, 8), 96)], aother, ssend, srecv, sib)
    mine = aimg.at[pl.ds(brow, 96)]
    pltpu.make_async_copy(mine, a_out.at[c], outsem.at[2]).start()
    for a in range(2):
        got(rbuf.at[other, pl.ds(0, 16), strip(a)], drecv.at[a])
    pltpu.make_async_copy(rbuf, r_out, outsem.at[1]).start()
    got(aother, srecv)
    pltpu.make_async_copy(aother, a_out.at[other], outsem.at[3]).start()

    for i, (src, dst) in enumerate(((bwhole, b_out), (rbuf, r_out), (mine, a_out.at[c]), (aother, a_out.at[other]))):
        pltpu.make_async_copy(src, dst, outsem.at[i]).wait()
    got(bst, wsend)
    got(afull.at[pl.ds(0, 672)], asend)
    got(own_m, msend)
    got(bbuf.at[pl.ds(0, 31)], gsend)
    got(bbuf.at[pl.ds(0, 31)], rsend)
    got(bslots.at[pl.ds(1, 7)], bsend)
    got(obf.at[pl.ds(0, 15)], osend1)
    got(obf.at[pl.ds(0, 7)], osend2)
    got(obf.at[pl.ds(0, 15)], osend4)
    got(rbuf.at[c], dsend)
    got(aother, ssend)


def last_kernel(
    r_hbm, b_hbm, a_hbm, oa_hbm, ob_hbm, oo_hbm, r_ref, b_ref, a_ref, oa_ref, ob_ref, oo_ref, insem, outsem
):
    factor = 1.0 / math.sqrt(512)
    loads = [
        pltpu.make_async_copy(src, dst, insem.at[i])
        for i, (src, dst) in enumerate(((r_hbm, r_ref), (b_hbm, b_ref), (a_hbm, a_ref)))
    ]
    for load in loads:
        load.start()
    stores = []

    def store(src, dst):
        stores.append(pltpu.make_async_copy(src, dst, outsem.at[len(stores)]))
        stores[-1].start()

    loads[0].wait()
    for g in range(2):
        rows = pl.ds(BLK * g, BLK)
        for h in range(2):
            oo_ref[rows, h * BLK:(h + 1) * BLK] = r_ref[h, 8 * g:8 * g + 8].reshape(BLK, BLK).astype(F32)
        store(oo_ref.at[rows], oo_hbm.at[rows])
    loads[1].wait()
    res_a = 0.0
    for h in range(2):
        half = r_ref[h].reshape(512, BLK)
        for v in split(b_ref[h]):
            res_a += lax.dot_general(v, half, (((1,), (1,)), ((), ())), preferred_element_type=F32)
    oa_ref[...] = (res_a * factor).astype(BF16)
    store(oa_ref, oa_hbm)
    loads[2].wait()
    res_b = [0.0, 0.0]
    for h in range(2):
        for v in split(a_ref[h]):
            for j in range(2):
                rows = r_ref[j, 8 * h:8 * h + 8].reshape(BLK, BLK)
                res_b[j] += jnp.dot(v, rows, preferred_element_type=F32)
    for j in range(2):
        ob_ref[:, j * BLK:(j + 1) * BLK] = (res_b[j] * factor).astype(BF16)
    store(ob_ref, ob_hbm)
    for copy in stores:
        copy.wait()


def local(margin, margin_pattern, orbitals_a, pattern_a, orbitals_b, pattern_b):
    smem, any_ = (pl.BlockSpec(memory_space=s) for s in (pltpu.SMEM, pl.ANY))
    dma = pltpu.SemaphoreType.DMA
    later = len(LATER)

    def buf(*shape, dtype=BF16):
        return pltpu.VMEM(shape, dtype)

    middle = pl.pallas_call(
        kernel,
        out_shape=(
            jax.ShapeDtypeStruct((2, 16, 32, 256), BF16),
            jax.ShapeDtypeStruct((2, 96, 256), F32),
            jax.ShapeDtypeStruct((2, 96, 256), F32),
        ),
        in_specs=[any_, any_, any_, smem, any_, smem],
        out_specs=(any_, any_, any_),
        scratch_shapes=[
            buf(768, 6144), buf(768, 512), buf(512, 768), buf(32, 384, 128), buf(192, 128), buf(32, 384, 128),
            buf(32, ROWS0, 128), buf(8 * later, ROWS1, 128), buf(24 * later, ROWS1, 128), buf(7, ROWS0, 128),
            buf(768, 256, dtype=F32), buf(2, 4, 96, 256), buf(8, 96, 256),
            buf(16, 32, 256, dtype=F32), buf(16, 32, 256), buf(16, 32, 256),
            buf(8, 32, 256), buf(2, 16, 32, 256), buf(192, 256, dtype=F32), buf(96, 256, dtype=F32),
            buf(2, 96, 256, dtype=F32), buf(96, 512), buf(96, 512), pltpu.SMEM((96, 96), jnp.int32),
            dma, dma((3,)), dma, dma((4,)), dma, dma((8,)), dma, dma, dma, dma((CH * len(PART),)),
            dma, dma((32 + 8 * later,)), dma((24 * later,)), dma((4,)), dma, dma((8,)), dma, dma((32,)), dma, dma((16,)),
            dma, dma((32,)), dma, dma((2,)), dma, dma, dma((4,)),
        ],
        compiler_params=pltpu.CompilerParams(
            collective_id=0, has_side_effects=True, vmem_limit_bytes=60 << 20
        ),
        name="exchange",
    )(margin, margin_pattern, orbitals_a, pattern_a.T, orbitals_b, pattern_b.T)
    return pl.pallas_call(
        last_kernel,
        out_shape=(
            jax.ShapeDtypeStruct((96, 512), BF16),
            jax.ShapeDtypeStruct((96, 512), BF16),
            jax.ShapeDtypeStruct((512, 512), F32),
        ),
        in_specs=[any_, any_, any_],
        out_specs=(any_, any_, any_),
        scratch_shapes=[
            buf(2, 16, 32, 256), buf(2, 96, 256, dtype=F32), buf(2, 96, 256, dtype=F32),
            buf(96, 512), buf(96, 512), buf(512, 512, dtype=F32), dma((3,)), dma((4,)),
        ],
        compiler_params=pltpu.CompilerParams(vmem_limit_bytes=60 << 20),
        name="last",
    )(*middle)


def solution(mesh):
    in_specs = (P("row", "col"), P(), P(("row", "col"), None), P(), P(("col", "row"), None), P())
    out_specs = (P(("row", "col"), None), P(("col", "row"), None), P())
    return jax.shard_map(local, mesh=mesh, in_specs=in_specs, out_specs=out_specs, check_vma=False)
```

```python
import math

import jax
import jax.numpy as jnp
from jax import lax
from jax.experimental import pallas as pl
from jax.experimental.pallas import tpu as pltpu
from jax.sharding import PartitionSpec as P

MESH = pl.DeviceIdType.MESH
F32 = jnp.float32
BF16 = jnp.bfloat16
BLK = 256
NX, NY, NZ = 4, 4, 8
CH = NX * NZ
PART = ((0, 160), (160, 128), (288, 96))
USED = tuple(start // 2 for start, _ in PART)
LATER = range(1, len(PART))
ROWS0, ROWS1 = PART[0][1], max(rows for _, rows in PART[1:])
LEN = ((4, 3), (4, 3), (3, 4), (3, 4), (4, 3))

ORDER = (
    ("z1", 1, 0, 1), ("z1", 1, 1, 1), ("x0", 3), ("z1", 2, 1, 1), ("z1", 2, 0, 1), ("z0", 0, 0, 1), ("z0", 0, 1, 1),
    ("z1", 1, 0, 2), ("apass",), ("z1", 1, 1, 2), ("x1", 1, 0), ("x0", 1), ("x1", 1, -1), ("x1", 1, 1),
    ("z1", 2, 0, 2), ("x1", 2, 1), ("z0", 3, 0, 1), ("z0", 3, 1, 1), ("z1", 2, 1, 2), ("x0", 2), ("x1", 2, 0),
    ("aturn",), ("terms", 0), ("x1", 1, -2), ("z1", 1, 1, 3), ("z0", 0, 0, 2), ("z1", 1, 0, 3), ("terms", 1),
    ("z1", 2, 0, 3), ("z0", 1, 0, 1), ("x1", 2, -1), ("z0", 1, 1, 1), ("terms", 2), ("z0", 3, 1, 2), ("x1", 1, 2),
    ("z0", 0, 1, 2), ("z1", 2, 1, 3), ("z0", 2, 0, 1), ("z0", 3, 0, 2), ("terms", 3), ("u", 1, 4), ("z0", 2, 1, 1),
    ("r0", 2, 1, 0), ("u", 2, 4), ("r0", 0, 0, 0), ("r0", 3, 1, 0), ("r0", 1, 0, 0), ("x1", 2, 2), ("z1", 2, 0, 4),
    ("x1", 1, 3), ("u", 2, -3), ("z1", 1, 0, 4), ("x1", 2, -2), ("z0", 3, 1, 3), ("x1", 2, -3), ("z0", 1, 0, 2),
    ("x1", 1, -3), ("z0", 2, 1, 2), ("z0", 0, 0, 3), ("r0", 3, 0, 0), ("upass", 2, 4), ("upass", 1, 4),
    ("r0", 2, 1, 1), ("x1", 2, 3), ("u", 1, -3), ("x1", 2, -4), ("u", 1, 3), ("z0", 1, 1, 2), ("z0", 2, 0, 2),
    ("bpart", 0), ("u", 2, 3), ("r0", 1, 1, 0), ("z0", 1, 0, 3), ("r0", 2, 0, 0), ("x1", 1, -4), ("u", 1, -2),
    ("z0", 3, 1, 4), ("z0", 0, 1, 3), ("z0", 0, 0, 4), ("r0", 1, 0, 1), ("u", 2, -1), ("z0", 3, 0, 3),
    ("z0", 2, 1, 3), ("r0", 3, 1, 1), ("r0", 0, 0, 1), ("upass", 2, -3), ("bpart", 1), ("r0", 3, 0, 1),
    ("upass", 1, -3), ("r0", 0, 1, 0), ("z0", 2, 0, 3), ("u", 1, 2), ("u", 2, -2), ("u", 1, -1), ("r0", 2, 1, 2),
    ("r1", 2, 0, 0), ("upass", 1, 3), ("z0", 1, 1, 3), ("u", 2, 2), ("z0", 1, 0, 4), ("r0", 1, 1, 1), ("r1", 1, 0, 0),
    ("upass", 2, 3), ("bpart", 2), ("z0", 2, 1, 4), ("r0", 2, 0, 1), ("bpart", 3), ("r0", 1, 0, 2), ("r0", 3, 1, 2),
    ("upass", 1, -2), ("orb", 0), ("orb", 1), ("r0", 3, 0, 2), ("r0", 2, 1, 3), ("u", 2, 1), ("r0", 1, 1, 2),
    ("r0", 0, 0, 2), ("r1", 1, 0, 1), ("r1", 2, 1, 0), ("u", 2, 0), ("upass", 2, -2), ("upass", 1, 2),
    ("upass", 2, 2), ("u", 1, 0), ("u", 1, 1), ("r1", 1, 1, 0), ("r0", 2, 0, 2), ("r0", 0, 1, 1), ("r0", 1, 0, 3),
    ("r0", 3, 1, 3), ("r1", 2, 0, 1), ("orb2", 0), ("upass", 1, -1), ("orb2", 1), ("r0x", 2), ("r1", 2, 1, 1),
    ("r0x", 1), ("upass", 2, 1), ("upass", 2, -1), ("upass", 2, 0), ("upass", 1, 1), ("r1", 2, 0, 2), ("r1", 1, 1, 1),
    ("r1", 1, 0, 2), ("r0", 0, 0, 3), ("upass", 1, 0), ("r0", 0, 1, 2), ("r0x", 3), ("orb4", 0), ("r1", 2, 1, 2),
    ("orb4", 1), ("r1", 2, 0, 3), ("r1", 1, 0, 3), ("r1", 1, 1, 2), ("end0",), ("orbend", 0), ("end1", 2),
    ("end1", 1), ("orbend", 1),
)


def up(v, n):
    return lax.rem(v, n)


def spots(core, block):
    found = []
    for (start, rows), used in zip(PART, USED):
        low, high = max(used, 96 * block), min(used + rows // 2, 96 * block + 96)
        if low < high:
            found.append((start + core * rows // 2 + low - used, high - low))
    return found


def contract0(a, b):
    return lax.dot_general(a, b, (((0,), (0,)), ((), ())), preferred_element_type=F32)


def split(v):
    high = v.astype(BF16)
    return high, (v - high.astype(F32)).astype(BF16)


def kernel(
    m_ref, pm_hbm, a_hbm, pa_hbm, b_hbm, pb_hbm,
    r_out, b_out, a_out,
    mbuf, afull, at, bbuf, bst, terms, zbuf, zbuf1, ubuf, xbuf, bacc, bpart, bslots,
    of32, obf, ar1, az, rbuf, aimg, bwhole, a_ref, b_ref, pm_ref, pa_ref, pb_ref,
    lsem, insem, msend, mrecv, asend, arecv, wsend, wrecv, gsend, grecv,
    rsend, zrecv, urecv, xrecv, bsend, brecv, osend1, orecv1, osend2, orecv2,
    osend4, orecv4, dsend, drecv, ssend, srecv, outsem,
):
    r = lax.axis_index("row")
    y = lax.axis_index("col")
    x, z, c = r // (2 * NZ), (r // 2) % NZ, r % 2
    p = x * NZ + z

    def dev(dx, dz, dy, oc=None):
        core = c if oc is None else oc
        return (up(x + dx, NX) * (2 * NZ) + up(z + dz + NZ, NZ) * 2 + core, up(y + dy, NY))

    def chip(k, dz):
        return up(x + k, NX) * NZ + up(z + dz + NZ, NZ)

    def send(src, dst, ssem, rsem, to):
        pltpu.make_async_remote_copy(
            src_ref=src, dst_ref=dst, send_sem=ssem, recv_sem=rsem, device_id=to, device_id_type=MESH
        ).start()

    def got(dst, sem):
        pltpu.make_async_copy(dst, dst, sem).wait()

    other = 1 - c
    sib = dev(0, 0, 0, other)
    zup, zdown = dev(0, 1, 0), dev(0, -1, 0)

    partners = [sib] + [dev(0, 0, k) for k in (1, 2, 3)]
    for core in (c, other):
        partners += [dev(0, 1, 0, core), dev(0, -1, 0, core)] + [dev(k, 0, 0, core) for k in (1, 2, 3)]
    bar = pltpu.get_barrier_semaphore()
    for to in partners:
        pl.semaphore_signal(bar, inc=1, device_id=to, device_id_type=MESH)
    loads = []
    staged = ((b_hbm, b_ref), (a_hbm, a_ref), (pm_hbm, pm_ref), (pb_hbm, pb_ref), (pa_hbm, pa_ref))
    for i, (src, dst) in enumerate(staged):
        loads.append(pltpu.make_async_copy(src, dst, insem.at[i]))
        loads[-1].start()
    own_m = mbuf.at[pl.ds(pl.multiple_of(c * 384, 128), 384)]
    local = pltpu.make_async_copy(m_ref, own_m, lsem)
    local.start()

    def masked(ref, pat, d):
        first, last = (96 * d) // BLK, (96 * d + 95) // BLK
        rows = 96 * d + lax.broadcasted_iota(jnp.int32, (96, BLK), 0)
        inside = rows < (first + 1) * BLK
        parts = []
        for k in range(2):
            keep = jnp.where(inside, pat[k, first].astype(F32), pat[k, last].astype(F32))
            parts.append((ref[:, k * BLK:(k + 1) * BLK].astype(F32) * keep).astype(BF16))
        return parts

    loads[0].wait()
    loads[3].wait()
    b0, b1 = masked(b_ref, pb_ref, 64 * y + r)
    here = jnp.where(c == 0, b0.astype(F32), b1.astype(F32)).astype(BF16)
    there = jnp.where(c == 0, b1.astype(F32), b0.astype(F32)).astype(BF16)
    brow = pl.multiple_of(96 * c, 16)
    here = jnp.concatenate([here[:, 0:128], here[:, 128:256]], axis=0)
    bst[...] = jnp.concatenate([there[:, 0:128], there[:, 128:256]], axis=0)

    def own_piece(h):
        start, rows = PART[h]
        return bbuf.at[p, pl.ds(pl.multiple_of(start + c * (rows // 2), 16), rows // 2)]

    def other_piece(h):
        return bst.at[pl.ds(USED[h], PART[h][1] // 2)]

    for h in range(len(PART)):
        own_piece(h)[...] = here[USED[h]:USED[h] + PART[h][1] // 2, :]
    loads[1].wait()
    loads[4].wait()
    arow = pl.multiple_of(384 * c + 96 * y, 16)
    a0, a1 = masked(a_ref, pa_ref, 4 * r + y)
    afull[pl.ds(arow, 96), 0:256] = a0
    afull[pl.ds(arow, 96), 256:512] = a1
    pl.semaphore_wait(bar, len(partners))

    def chunk(h, idx):
        return bbuf.at[idx, pl.ds(*PART[h])]

    def gsend_to(h, idx, to):
        send(chunk(h, idx), chunk(h, idx), gsend, grecv.at[h * CH + idx], to)

    def gwait(h, idx):
        got(chunk(h, idx), grecv.at[h * CH + idx])

    def first_send(h, dx, dz):
        send(own_piece(h), own_piece(h), gsend, grecv.at[h * CH + p], dev(dx, dz, 0))
        send(other_piece(h), own_piece(h), gsend, grecv.at[h * CH + p], dev(dx, dz, 0, other))

    for h in LATER:
        first_send(h, 0, 1)
        first_send(h, 0, -1)
    for k in (1, 3, 2):
        first_send(0, k, 0)
    first_send(0, 0, 1)
    first_send(0, 0, -1)
    for h in LATER:
        for k in (1, 3):
            first_send(h, k, 0)
    for h in range(len(PART)):
        send(other_piece(h), own_piece(h), wsend, wrecv, sib)

    def a_rows(core, dy):
        return afull.at[pl.ds(pl.multiple_of(384 * core + 96 * up(y + NY - dy, NY), 16), 96)]

    own_a = a_rows(c, 0)
    send(own_a, own_a, asend, arecv.at[4], sib)
    for dy in (1, 3, 2):
        send(own_a, own_a, asend, arecv.at[dy], dev(0, 0, dy))

    def margin_piece(i):
        def body(t, carry):
            j = 6 * i + t
            cols = pl.ds(pl.multiple_of(BLK * j, BLK), BLK)
            for e in range(3):
                rows = pl.ds(pl.multiple_of(384 * c + 128 * e, 128), 128)
                keep = pm_ref[3 * p + (3 * c + e) // 2, 24 * y + j].astype(F32)
                mbuf[rows, cols] = mbuf[rows, cols] * jnp.full((128, BLK), keep, F32).astype(BF16)
            return carry

        lax.fori_loop(0, 6, body, 0)
        piece = mbuf.at[pl.ds(pl.multiple_of(384 * c, 128), 384), pl.ds(1536 * i, 1536)]
        send(piece, piece, msend, mrecv.at[i], sib)

    local.wait()
    loads[2].wait()
    margin_piece(0)
    margin_piece(1)

    margin_piece(2)
    margin_piece(3)

    def do_x0(k):
        gwait(0, chip(k, 0))
        gsend_to(0, chip(k, 0), zup)
        gsend_to(0, chip(k, 0), zdown)

    def do_z0(k, way, s):
        idx = chip(k, s if way else -s)
        gwait(0, idx)
        if s < LEN[k][way]:
            gsend_to(0, idx, zdown if way else zup)

    def do_z1(h, way, s):
        idx = chip(0, s if way else -s)
        gwait(h, idx)
        if s < LEN[4][way]:
            gsend_to(h, idx, zdown if way else zup)
        for k in (1, 3):
            gsend_to(h, idx, dev(k, 0, 0))

    def offsets(s):
        return (0,) if s == 0 else (-s, s) if s < 4 else (-s,)

    def do_x1(h, off):
        odd_chunk = (z + off + NZ) % 2
        gwait(h, chip(1, off))
        gwait(h, chip(3, off))
        gsend_to(h, chip(3 - 2 * odd_chunk, off), dev(1 + 2 * odd_chunk, 0, 0))

    def gather_last(s):
        for off in offsets(s):
            for h in LATER:
                gwait(h, chip(2, off))

    ccol = pl.multiple_of(c * BLK, BLK)

    def term_body(q, carry):
        cols = pl.ds(pl.multiple_of(q * 768, 128), 768)
        both = jnp.dot(at[pl.ds(ccol, BLK), :], mbuf[:, cols], preferred_element_type=F32)
        low_lanes = lax.broadcasted_iota(jnp.int32, (64, 128), 1) < 64
        for u in range(4):
            h, pair = u % 2, u // 2
            whole = both[128 * h:128 * h + 128, 384 * pair:384 * pair + 384]
            top, bottom = whole[0:64, 128:256], whole[64:128, 128:256]
            first = jnp.where(low_lanes, top, pltpu.roll(bottom, 64, 1))
            second = jnp.where(low_lanes, pltpu.roll(top, 64, 1), bottom)
            for e, (tile_e, rest) in enumerate(((whole[:, 0:128], first), (whole[:, 256:384], second))):
                chunk_at = 4 * q + 2 * pair + e
                terms[chunk_at, 192 * h:192 * h + 128, :] = tile_e.astype(BF16)
                terms[chunk_at, 192 * h + 128:192 * h + 192, :] = rest.astype(BF16)
        return carry

    halfz, odd = z // 2, z % 2

    def do_terms(i):
        if i == 0:
            for j in range(4):
                got(mbuf.at[pl.ds(pl.multiple_of(384 * other, 128), 384), pl.ds(1536 * j, 1536)], mrecv.at[j])
        lax.fori_loop(2 * i, 2 * i + 2, term_body, 0)

    def do_bpart(i):
        if i == 0:
            got(bst, wrecv)
            gather_last(0)
        gather_last(i + 1)
        shift = (0, 3 + 2 * odd, 1 + 2 * odd, 2)[i]
        pair = up(halfz + shift, NZ // 2)
        tiles, rows = [], []
        for k in range(NX):
            first = up(x + k, NX) * NZ + 2 * pair
            tiles.append(mbuf[:, pl.ds(pl.multiple_of(192 * first, 128), 384)])
            halves = []
            for block in range(2):
                found = [(e, spot) for e in range(2) for core in range(2) for spot in spots(core, block)]
                halves.append(jnp.concatenate([bbuf[first + e, a:a + n, :] for e, (a, n) in found], axis=0))
            rows.append(jnp.concatenate(halves, axis=1))
        part = jnp.dot(
            jnp.concatenate(tiles, axis=1), jnp.concatenate(rows, axis=0), preferred_element_type=F32
        )
        bacc[...] = part if i == 0 else bacc[...] + part

    def do_apass():
        for dy in (1, 3, 2):
            got(a_rows(c, dy), arecv.at[dy])
            send(a_rows(c, dy), a_rows(c, dy), asend, arecv.at[4 + dy], sib)

    def do_aturn():
        for dy in (0, 1, 3, 2):
            got(a_rows(other, dy), arecv.at[4 + dy])
        at[...] = afull[...].T

    def t_at(h, idx):
        return terms.at[idx, pl.ds(*PART[h])]

    def t_val(h, idx):
        return terms[idx, pl.ds(*PART[h]), :].astype(F32)

    order = (4, -3, 3, -2, 2, -1, 1, 0)

    def ways(off):
        odd_chunk = (z + off + NZ) % 2
        return 1 + 2 * odd_chunk, 3 - 2 * odd_chunk

    def uref(h, off, j):
        i = 24 * (h - 1) + 3 * order.index(off) + j
        return ubuf.at[i, pl.ds(0, PART[h][1])], urecv.at[i]

    def usend(src, h, off, j, k):
        dst, sem = uref(h, off, j)
        send(src, dst, rsend, sem, dev(k, 0, 0))

    def do_u(h, off):
        ahead, back = ways(off)
        usend(t_at(h, chip(2, off)), h, off, 0, ahead)
        usend(t_at(h, chip(back, off)), h, off, 1, back)

    def do_upass(h, off):
        ahead, _ = ways(off)
        ref, sem = uref(h, off, 0)
        got(ref, sem)
        ref[...] = (ref[...].astype(F32) + t_val(h, chip(ahead, off))).astype(BF16)
        usend(ref, h, off, 2, ahead)

    def usum(h, off):
        total = t_val(h, chip(0, off))
        for j in (1, 2):
            ref, sem = uref(h, off, j)
            got(ref, sem)
            total += ref[...].astype(F32)
        return total

    def zref(h, k, way, s):
        if h:
            slot = 8 * (h - 1) + 4 * way + s
            return zbuf1.at[slot, pl.ds(0, PART[h][1])], zrecv.at[32 + slot]
        slot = 8 * k + 4 * way + s
        return zbuf.at[slot], zrecv.at[slot]

    def zsend(src, h, k, way, s):
        dst, sem = zref(h, k, way, s)
        send(src, dst, rsend, sem, zup if way == 0 else zdown)

    def do_r0(k, way, s):
        lim = LEN[k][way]
        idx = chip(k, (s - lim) if way else (lim - s))
        if s == 0:
            zsend(t_at(0, idx), 0, k, way, 0)
        else:
            ref, sem = zref(0, k, way, s - 1)
            got(ref, sem)
            ref[...] = (ref[...].astype(F32) + t_val(0, idx)).astype(BF16)
            zsend(ref, 0, k, way, s)

    def do_r1(h, way, s):
        lim = LEN[4][way]
        off = (s - lim) if way else (lim - s)
        total = usum(h, off)
        if s > 0:
            ref, sem = zref(h, 4, way, s - 1)
            got(ref, sem)
            total += ref[...].astype(F32)
        mine = uref(h, off, 1)[0]
        mine[...] = total.astype(BF16)
        zsend(mine, h, 4, way, s)

    def plane():
        return [(4 * dx + dy, dx, dy) for dx in range(NX) for dy in range(NY) if dx or dy]

    def strip(a):
        return pl.ds(16 * a, 16)

    def do_orb(a):
        if a == 0:
            b_all = bacc[...]
            high = b_all.astype(BF16)
            low = (b_all - high.astype(F32)).astype(BF16)
            bpart[...] = high.reshape(2, NY, 96, BLK)
            orb = jnp.dot(at[...], high, preferred_element_type=F32)
            orb += jnp.dot(at[...], low, preferred_element_type=F32)
            orb = orb.reshape(16, 32, BLK)
            of32[...] = orb
            obf[...] = orb.astype(BF16)
        for slot, dx, dy in plane():
            src = obf.at[up(x + dx, NX) * 4 + up(y + dy, NY), strip(a)]
            send(src, ar1.at[slot, strip(a)], osend1, orecv1.at[16 * a + slot], dev(dx, 0, dy))
        if a == 1:
            for dy in range(NY):
                for oc in range(2):
                    if dy or oc:
                        core = c if oc == 0 else other
                        slot = 2 * dy + oc
                        src = bpart.at[core, up(y + dy, NY)]
                        send(src, bslots.at[slot], bsend, brecv.at[slot], dev(0, 0, dy, core))
            bslots[0] = bpart[c, y]

    def do_orb2(a):
        total = of32[4 * x + y, strip(a), :]
        for slot, _, _ in plane():
            got(ar1.at[slot, strip(a)], orecv1.at[16 * a + slot])
            total += ar1[slot, strip(a), :].astype(F32)
        mine = az.at[z, strip(a)]
        mine[...] = total.astype(BF16)
        for dz in (4, 3, 5, 2, 6, 1, 7):
            send(mine, mine, osend2, orecv2.at[8 * a + dz], dev(0, dz, 0))

    def do_orb4(a):
        for dz in range(1, NZ):
            got(az.at[up(z - dz + NZ, NZ), strip(a)], orecv2.at[8 * a + dz])
        total = az[0, strip(a), :].astype(F32)
        for i in range(1, NZ):
            total += az[i, strip(a), :].astype(F32)
        mine = rbuf.at[c, 4 * x + y, strip(a)]
        mine[...] = (total * (1.0 / math.sqrt(24576))).astype(BF16)
        for slot, dx, dy in plane():
            send(mine, mine, osend4, orecv4.at[16 * a + slot], dev(dx, 0, dy))

    def zlast(h, k):
        total = usum(h, 0) if h else t_val(0, chip(k, 0))
        for way in range(2):
            ref, sem = zref(h, k, way, LEN[k][way] - 1)
            got(ref, sem)
            total += ref[...].astype(F32)
        return total

    def do_r0x(k):
        xbuf[k] = zlast(0, k).astype(BF16)
        send(xbuf.at[k], xbuf.at[3 + k], rsend, xrecv.at[k], dev(k, 0, 0))

    pieces = {}

    def do_end0():
        total = zlast(0, 0)
        for k in (1, 3, 2):
            got(xbuf.at[3 + k], xrecv.at[k])
            total += xbuf[3 + k].astype(F32)
        pieces[0] = total
        for oc in range(2):
            total = 0.0
            for dy in range(NY):
                slot = 2 * dy + oc
                if slot:
                    got(bslots.at[slot], brecv.at[slot])
                total += bslots[slot].astype(F32)
            bwhole[c if oc == 0 else other] = total
        pltpu.make_async_copy(bwhole, b_out, outsem.at[3]).start()

    def do_end1(h):
        pieces[h] = zlast(h, 4)

    def do_orbend(a):
        for slot, dx, dy in plane():
            src = up(x - dx + NX, NX) * 4 + up(y - dy + NY, NY)
            got(rbuf.at[c, src, strip(a)], orecv4.at[16 * a + slot])
        half, there = rbuf.at[c, pl.ds(0, 16), strip(a)], r_out.at[c, pl.ds(0, 16), strip(a)]
        send(half, there, dsend, drecv.at[a], sib)
        pltpu.make_async_copy(half, there, outsem.at[a]).start()

    steps = dict(
        x0=do_x0, z0=do_z0, z1=do_z1, x1=do_x1, apass=do_apass, aturn=do_aturn, terms=do_terms, bpart=do_bpart,
        u=do_u, upass=do_upass, r0=do_r0, r1=do_r1, r0x=do_r0x, orb=do_orb, orb2=do_orb2, orb4=do_orb4,
        orbend=do_orbend, end0=do_end0, end1=do_end1,
    )
    for name, *where in ORDER:
        steps[name](*where)

    image = jnp.concatenate([pieces[h] for h in range(len(PART))], axis=0)
    for h in range(2):
        lanes = pl.ds(128 * h, 128)
        packed = image[192 * h + 128:192 * h + 192, :]
        rest = jnp.concatenate([packed, pltpu.roll(packed, 64, 1)], axis=0).T
        aimg[pl.ds(pl.multiple_of(64 * odd, 8), 128), lanes] = image[192 * h:192 * h + 128, :].T
        aimg[pl.ds(pl.multiple_of(128 * (1 - odd), 8), 64), lanes] = rest[0:64, :]
    send(aimg.at[pl.ds(pl.multiple_of(96 * other, 8), 96)], a_out.at[c], ssend, srecv, sib)
    mine = aimg.at[pl.ds(brow, 96)]
    pltpu.make_async_copy(mine, a_out.at[c], outsem.at[2]).start()
    for a in range(2):
        got(r_out.at[other, pl.ds(0, 16), strip(a)], drecv.at[a])
        got(r_out.at[c, pl.ds(0, 16), strip(a)], outsem.at[a])
    got(bwhole, outsem.at[3])
    got(mine, outsem.at[2])

    got(bst, wsend)
    got(afull.at[pl.ds(0, 672)], asend)
    got(own_m, msend)
    got(bbuf.at[pl.ds(0, 31)], gsend)
    got(bbuf.at[pl.ds(0, 31)], rsend)
    got(bslots.at[pl.ds(1, 7)], bsend)
    got(obf.at[pl.ds(0, 15)], osend1)
    got(obf.at[pl.ds(0, 7)], osend2)
    got(obf.at[pl.ds(0, 15)], osend4)
    got(rbuf.at[c], dsend)
    got(mine, ssend)
    got(a_out.at[other], srecv)


def last_kernel(
    r_hbm, b_hbm, a_hbm, oa_hbm, ob_hbm, oo_hbm, r_ref, b_ref, a_ref, oa_ref, ob_ref, oo_ref, insem, outsem
):
    factor = 1.0 / math.sqrt(512)
    loads = [
        pltpu.make_async_copy(src, dst, insem.at[i])
        for i, (src, dst) in enumerate(((r_hbm, r_ref), (b_hbm, b_ref), (a_hbm, a_ref)))
    ]
    for load in loads:
        load.start()
    stores = []

    def store(src, dst):
        stores.append(pltpu.make_async_copy(src, dst, outsem.at[len(stores)]))
        stores[-1].start()

    loads[0].wait()
    for g in range(2):
        rows = pl.ds(BLK * g, BLK)
        for h in range(2):
            oo_ref[rows, h * BLK:(h + 1) * BLK] = r_ref[h, 8 * g:8 * g + 8].reshape(BLK, BLK).astype(F32)
        store(oo_ref.at[rows], oo_hbm.at[rows])
    loads[1].wait()
    res_a = 0.0
    for h in range(2):
        half = r_ref[h].reshape(512, BLK)
        for v in split(b_ref[h]):
            res_a += lax.dot_general(v, half, (((1,), (1,)), ((), ())), preferred_element_type=F32)
    oa_ref[...] = (res_a * factor).astype(BF16)
    store(oa_ref, oa_hbm)
    loads[2].wait()
    res_b = [0.0, 0.0]
    for h in range(2):
        for v in split(a_ref[h]):
            for j in range(2):
                rows = r_ref[j, 8 * h:8 * h + 8].reshape(BLK, BLK)
                res_b[j] += jnp.dot(v, rows, preferred_element_type=F32)
    for j in range(2):
        ob_ref[:, j * BLK:(j + 1) * BLK] = (res_b[j] * factor).astype(BF16)
    store(ob_ref, ob_hbm)
    for copy in stores:
        copy.wait()


def local(margin, margin_pattern, orbitals_a, pattern_a, orbitals_b, pattern_b):
    any_ = pl.BlockSpec(memory_space=pl.ANY)
    dma = pltpu.SemaphoreType.DMA
    later = len(LATER)

    def buf(*shape, dtype=BF16):
        return pltpu.VMEM(shape, dtype)

    middle = pl.pallas_call(
        kernel,
        out_shape=(
            jax.ShapeDtypeStruct((2, 16, 32, 256), BF16),
            jax.ShapeDtypeStruct((2, 96, 256), F32),
            jax.ShapeDtypeStruct((2, 96, 256), F32),
        ),
        in_specs=[any_] * 6,
        out_specs=(any_, any_, any_),
        scratch_shapes=[
            buf(768, 6144), buf(768, 512), buf(512, 768), buf(32, 384, 128), buf(192, 128), buf(32, 384, 128),
            buf(32, ROWS0, 128), buf(8 * later, ROWS1, 128), buf(24 * later, ROWS1, 128), buf(7, ROWS0, 128),
            buf(768, 256, dtype=F32), buf(2, 4, 96, 256), buf(8, 96, 256),
            buf(16, 32, 256, dtype=F32), buf(16, 32, 256), buf(16, 32, 256),
            buf(8, 32, 256), buf(2, 16, 32, 256), buf(192, 256, dtype=F32),
            buf(2, 96, 256, dtype=F32), buf(96, 512), buf(96, 512), pltpu.SMEM((96, 96), jnp.int32),
            pltpu.SMEM((2, 96), jnp.int32), pltpu.SMEM((2, 96), jnp.int32),
            dma, dma((5,)), dma, dma((4,)), dma, dma((8,)), dma, dma, dma, dma((CH * len(PART),)),
            dma, dma((32 + 8 * later,)), dma((24 * later,)), dma((4,)), dma, dma((8,)), dma, dma((32,)), dma, dma((16,)),
            dma, dma((32,)), dma, dma((2,)), dma, dma, dma((4,)),
        ],
        compiler_params=pltpu.CompilerParams(
            collective_id=0, has_side_effects=True, vmem_limit_bytes=60 << 20
        ),
        name="exchange",
    )(margin, margin_pattern, orbitals_a, pattern_a.T, orbitals_b, pattern_b.T)
    return pl.pallas_call(
        last_kernel,
        out_shape=(
            jax.ShapeDtypeStruct((96, 512), BF16),
            jax.ShapeDtypeStruct((96, 512), BF16),
            jax.ShapeDtypeStruct((512, 512), F32),
        ),
        in_specs=[any_, any_, any_],
        out_specs=(any_, any_, any_),
        scratch_shapes=[
            buf(2, 16, 32, 256), buf(2, 96, 256, dtype=F32), buf(2, 96, 256, dtype=F32),
            buf(96, 512), buf(96, 512), buf(512, 512, dtype=F32), dma((3,)), dma((4,)),
        ],
        compiler_params=pltpu.CompilerParams(vmem_limit_bytes=60 << 20),
        name="last",
    )(*middle)


def solution(mesh):
    in_specs = (P("row", "col"), P(), P(("row", "col"), None), P(), P(("col", "row"), None), P())
    out_specs = (P(("row", "col"), None), P(("col", "row"), None), P())
    return jax.shard_map(local, mesh=mesh, in_specs=in_specs, out_specs=out_specs, check_vma=False)
```

```python
import math

import jax
import jax.numpy as jnp
from jax import lax
from jax.experimental import pallas as pl
from jax.experimental.pallas import tpu as pltpu
from jax.sharding import PartitionSpec as P

MESH = pl.DeviceIdType.MESH
F32 = jnp.float32
BF16 = jnp.bfloat16
BLK = 256
NX, NY, NZ = 4, 4, 8
CH = NX * NZ
PART = ((0, 160), (160, 128), (288, 96))
USED = tuple(start // 2 for start, _ in PART)
LATER = range(1, len(PART))
ROWS0, ROWS1 = PART[0][1], max(rows for _, rows in PART[1:])
LEN = ((4, 3), (4, 3), (3, 4), (3, 4), (4, 3))

ORDER = (
    ("z1", 1, 0, 1), ("z1", 1, 1, 1), ("x0", 3), ("z1", 2, 1, 1), ("z1", 2, 0, 1), ("z0", 0, 0, 1), ("z0", 0, 1, 1),
    ("z1", 1, 0, 2), ("apass",), ("z1", 1, 1, 2), ("x1", 1, 0), ("x0", 1), ("x1", 1, -1), ("x1", 1, 1),
    ("z1", 2, 0, 2), ("x1", 2, 1), ("z0", 3, 0, 1), ("z0", 3, 1, 1), ("z1", 2, 1, 2), ("x0", 2), ("x1", 2, 0),
    ("aturn",), ("terms", 0), ("x1", 1, -2), ("z1", 1, 1, 3), ("z0", 0, 0, 2), ("z1", 1, 0, 3), ("terms", 1),
    ("z1", 2, 0, 3), ("z0", 1, 0, 1), ("x1", 2, -1), ("z0", 1, 1, 1), ("terms", 2), ("z0", 3, 1, 2), ("x1", 1, 2),
    ("z0", 0, 1, 2), ("z1", 2, 1, 3), ("z0", 2, 0, 1), ("z0", 3, 0, 2), ("terms", 3), ("u", 1, 4), ("z0", 2, 1, 1),
    ("r0", 2, 1, 0), ("u", 2, 4), ("r0", 0, 0, 0), ("r0", 3, 1, 0), ("r0", 1, 0, 0), ("x1", 2, 2), ("z1", 2, 0, 4),
    ("x1", 1, 3), ("u", 2, -3), ("z1", 1, 0, 4), ("x1", 2, -2), ("z0", 3, 1, 3), ("x1", 2, -3), ("z0", 1, 0, 2),
    ("x1", 1, -3), ("z0", 2, 1, 2), ("z0", 0, 0, 3), ("r0", 3, 0, 0), ("upass", 2, 4), ("upass", 1, 4),
    ("r0", 2, 1, 1), ("x1", 2, 3), ("u", 1, -3), ("x1", 2, -4), ("u", 1, 3), ("z0", 1, 1, 2), ("z0", 2, 0, 2),
    ("bpart", 0), ("u", 2, 3), ("r0", 1, 1, 0), ("z0", 1, 0, 3), ("r0", 2, 0, 0), ("x1", 1, -4), ("u", 1, -2),
    ("z0", 3, 1, 4), ("z0", 0, 1, 3), ("z0", 0, 0, 4), ("r0", 1, 0, 1), ("u", 2, -1), ("z0", 3, 0, 3),
    ("z0", 2, 1, 3), ("r0", 3, 1, 1), ("r0", 0, 0, 1), ("upass", 2, -3), ("bpart", 1), ("r0", 3, 0, 1),
    ("upass", 1, -3), ("r0", 0, 1, 0), ("z0", 2, 0, 3), ("u", 1, 2), ("u", 2, -2), ("u", 1, -1), ("r0", 2, 1, 2),
    ("r1", 2, 0, 0), ("upass", 1, 3), ("z0", 1, 1, 3), ("u", 2, 2), ("z0", 1, 0, 4), ("r0", 1, 1, 1), ("r1", 1, 0, 0),
    ("upass", 2, 3), ("bpart", 2), ("z0", 2, 1, 4), ("r0", 2, 0, 1), ("bpart", 3), ("r0", 1, 0, 2), ("r0", 3, 1, 2),
    ("upass", 1, -2), ("orb", 0), ("orb", 1), ("r0", 3, 0, 2), ("r0", 2, 1, 3), ("u", 2, 1), ("r0", 1, 1, 2),
    ("r0", 0, 0, 2), ("r1", 1, 0, 1), ("r1", 2, 1, 0), ("u", 2, 0), ("upass", 2, -2), ("upass", 1, 2),
    ("upass", 2, 2), ("u", 1, 0), ("u", 1, 1), ("r1", 1, 1, 0), ("r0", 2, 0, 2), ("r0", 0, 1, 1), ("r0", 1, 0, 3),
    ("r0", 3, 1, 3), ("r1", 2, 0, 1), ("orb2", 0), ("upass", 1, -1), ("orb2", 1), ("r0x", 2), ("r1", 2, 1, 1),
    ("r0x", 1), ("upass", 2, 1), ("upass", 2, -1), ("upass", 2, 0), ("upass", 1, 1), ("r1", 2, 0, 2), ("r1", 1, 1, 1),
    ("r1", 1, 0, 2), ("r0", 0, 0, 3), ("upass", 1, 0), ("r0", 0, 1, 2), ("r0x", 3), ("orb4", 0), ("r1", 2, 1, 2),
    ("orb4", 1), ("r1", 2, 0, 3), ("r1", 1, 0, 3), ("r1", 1, 1, 2), ("end0",), ("orbend", 0), ("end1", 2),
    ("end1", 1), ("orbend", 1),
)


def up(v, n):
    return lax.rem(v, n)


def spots(core, block):
    found = []
    for (start, rows), used in zip(PART, USED):
        low, high = max(used, 96 * block), min(used + rows // 2, 96 * block + 96)
        if low < high:
            found.append((start + core * rows // 2 + low - used, high - low))
    return found


def contract0(a, b):
    return lax.dot_general(a, b, (((0,), (0,)), ((), ())), preferred_element_type=F32)


def split(v):
    high = v.astype(BF16)
    return high, (v - high.astype(F32)).astype(BF16)


def kernel(
    m_ref, pm_hbm, a_hbm, pa_hbm, b_hbm, pb_hbm,
    r_out, b_out, a_out,
    mbuf, afull, at, bbuf, bst, terms, zbuf, zbuf1, ubuf, xbuf, bacc, bpart, bslots,
    of32, obf, ar1, az, rbuf, aimg, bwhole, a_ref, b_ref, pm_ref, pa_ref, pb_ref,
    lsem, insem, msend, mrecv, asend, arecv, wsend, wrecv, gsend, grecv,
    rsend, zrecv, urecv, xrecv, bsend, brecv, osend1, orecv1, osend2, orecv2,
    osend4, orecv4, dsend, drecv, ssend, srecv, outsem,
):
    r = lax.axis_index("row")
    y = lax.axis_index("col")
    x, z, c = r // (2 * NZ), (r // 2) % NZ, r % 2
    p = x * NZ + z

    def dev(dx, dz, dy, oc=None):
        core = c if oc is None else oc
        return (up(x + dx, NX) * (2 * NZ) + up(z + dz + NZ, NZ) * 2 + core, up(y + dy, NY))

    def chip(k, dz):
        return up(x + k, NX) * NZ + up(z + dz + NZ, NZ)

    def send(src, dst, ssem, rsem, to):
        pltpu.make_async_remote_copy(
            src_ref=src, dst_ref=dst, send_sem=ssem, recv_sem=rsem, device_id=to, device_id_type=MESH
        ).start()

    def got(dst, sem):
        pltpu.make_async_copy(dst, dst, sem).wait()

    other = 1 - c
    sib = dev(0, 0, 0, other)
    zup, zdown = dev(0, 1, 0), dev(0, -1, 0)

    partners = [sib] + [dev(0, 0, k) for k in (1, 2, 3)]
    for core in (c, other):
        partners += [dev(0, 1, 0, core), dev(0, -1, 0, core)] + [dev(k, 0, 0, core) for k in (1, 2, 3)]
    bar = pltpu.get_barrier_semaphore()
    for to in partners:
        pl.semaphore_signal(bar, inc=1, device_id=to, device_id_type=MESH)
    loads = []
    staged = ((b_hbm, b_ref), (a_hbm, a_ref), (pm_hbm, pm_ref), (pb_hbm, pb_ref), (pa_hbm, pa_ref))
    for i, (src, dst) in enumerate(staged):
        loads.append(pltpu.make_async_copy(src, dst, insem.at[i]))
        loads[-1].start()
    own_m = mbuf.at[pl.ds(pl.multiple_of(c * 384, 128), 384)]
    local = pltpu.make_async_copy(m_ref, own_m, lsem)
    local.start()

    def masked(ref, pat, d):
        first, last = (96 * d) // BLK, (96 * d + 95) // BLK
        rows = 96 * d + lax.broadcasted_iota(jnp.int32, (96, BLK), 0)
        inside = rows < (first + 1) * BLK
        parts = []
        for k in range(2):
            keep = jnp.where(inside, pat[k, first].astype(F32), pat[k, last].astype(F32))
            parts.append((ref[:, k * BLK:(k + 1) * BLK].astype(F32) * keep).astype(BF16))
        return parts

    loads[0].wait()
    loads[3].wait()
    b0, b1 = masked(b_ref, pb_ref, 64 * y + r)
    here = jnp.where(c == 0, b0.astype(F32), b1.astype(F32)).astype(BF16)
    there = jnp.where(c == 0, b1.astype(F32), b0.astype(F32)).astype(BF16)
    brow = pl.multiple_of(96 * c, 16)
    here = jnp.concatenate([here[:, 0:128], here[:, 128:256]], axis=0)
    bst[...] = jnp.concatenate([there[:, 0:128], there[:, 128:256]], axis=0)

    def own_piece(h):
        start, rows = PART[h]
        return bbuf.at[p, pl.ds(pl.multiple_of(start + c * (rows // 2), 16), rows // 2)]

    def other_piece(h):
        return bst.at[pl.ds(USED[h], PART[h][1] // 2)]

    for h in range(len(PART)):
        own_piece(h)[...] = here[USED[h]:USED[h] + PART[h][1] // 2, :]
    loads[1].wait()
    loads[4].wait()
    arow = pl.multiple_of(384 * c + 96 * y, 16)
    a0, a1 = masked(a_ref, pa_ref, 4 * r + y)
    afull[pl.ds(arow, 96), 0:256] = a0
    afull[pl.ds(arow, 96), 256:512] = a1
    pl.semaphore_wait(bar, len(partners))

    def chunk(h, idx):
        return bbuf.at[idx, pl.ds(*PART[h])]

    def gsend_to(h, idx, to):
        send(chunk(h, idx), chunk(h, idx), gsend, grecv.at[h * CH + idx], to)

    def gwait(h, idx):
        got(chunk(h, idx), grecv.at[h * CH + idx])

    def first_send(h, dx, dz):
        send(own_piece(h), own_piece(h), gsend, grecv.at[h * CH + p], dev(dx, dz, 0))
        send(other_piece(h), own_piece(h), gsend, grecv.at[h * CH + p], dev(dx, dz, 0, other))

    for h in LATER:
        first_send(h, 0, 1)
        first_send(h, 0, -1)
    for k in (1, 3, 2):
        first_send(0, k, 0)
    first_send(0, 0, 1)
    first_send(0, 0, -1)
    for h in LATER:
        for k in (1, 3):
            first_send(h, k, 0)
    for h in range(len(PART)):
        send(other_piece(h), own_piece(h), wsend, wrecv, sib)

    def a_rows(core, dy):
        return afull.at[pl.ds(pl.multiple_of(384 * core + 96 * up(y + NY - dy, NY), 16), 96)]

    own_a = a_rows(c, 0)
    send(own_a, own_a, asend, arecv.at[4], sib)
    for dy in (1, 3, 2):
        send(own_a, own_a, asend, arecv.at[dy], dev(0, 0, dy))

    def margin_piece(i):
        def body(t, carry):
            j = 6 * i + t
            cols = pl.ds(pl.multiple_of(BLK * j, BLK), BLK)
            for e in range(3):
                rows = pl.ds(pl.multiple_of(384 * c + 128 * e, 128), 128)
                keep = pm_ref[3 * p + (3 * c + e) // 2, 24 * y + j].astype(F32)
                mbuf[rows, cols] = mbuf[rows, cols] * jnp.full((128, BLK), keep, F32).astype(BF16)
            return carry

        lax.fori_loop(0, 6, body, 0)
        piece = mbuf.at[pl.ds(pl.multiple_of(384 * c, 128), 384), pl.ds(1536 * i, 1536)]
        send(piece, piece, msend, mrecv.at[i], sib)

    local.wait()
    loads[2].wait()
    margin_piece(0)
    margin_piece(1)

    margin_piece(2)
    margin_piece(3)

    def do_x0(k):
        gwait(0, chip(k, 0))
        gsend_to(0, chip(k, 0), zup)
        gsend_to(0, chip(k, 0), zdown)

    def do_z0(k, way, s):
        idx = chip(k, s if way else -s)
        gwait(0, idx)
        if s < LEN[k][way]:
            gsend_to(0, idx, zdown if way else zup)

    def do_z1(h, way, s):
        idx = chip(0, s if way else -s)
        gwait(h, idx)
        if s < LEN[4][way]:
            gsend_to(h, idx, zdown if way else zup)
        for k in (1, 3):
            gsend_to(h, idx, dev(k, 0, 0))

    def offsets(s):
        return (0,) if s == 0 else (-s, s) if s < 4 else (-s,)

    def do_x1(h, off):
        odd_chunk = (z + off + NZ) % 2
        gwait(h, chip(1, off))
        gwait(h, chip(3, off))
        gsend_to(h, chip(3 - 2 * odd_chunk, off), dev(1 + 2 * odd_chunk, 0, 0))

    def gather_last(s):
        for off in offsets(s):
            for h in LATER:
                gwait(h, chip(2, off))

    ccol = pl.multiple_of(c * BLK, BLK)

    def term_body(q, carry):
        cols = pl.ds(pl.multiple_of(q * 768, 128), 768)
        both = jnp.dot(at[pl.ds(ccol, BLK), :], mbuf[:, cols], preferred_element_type=F32)
        low_lanes = lax.broadcasted_iota(jnp.int32, (64, 128), 1) < 64
        for u in range(4):
            h, pair = u % 2, u // 2
            whole = both[128 * h:128 * h + 128, 384 * pair:384 * pair + 384]
            top, bottom = whole[0:64, 128:256], whole[64:128, 128:256]
            first = jnp.where(low_lanes, top, pltpu.roll(bottom, 64, 1))
            second = jnp.where(low_lanes, pltpu.roll(top, 64, 1), bottom)
            for e, (tile_e, rest) in enumerate(((whole[:, 0:128], first), (whole[:, 256:384], second))):
                chunk_at = 4 * q + 2 * pair + e
                terms[chunk_at, 192 * h:192 * h + 128, :] = tile_e.astype(BF16)
                terms[chunk_at, 192 * h + 128:192 * h + 192, :] = rest.astype(BF16)
        return carry

    halfz, odd = z // 2, z % 2

    def do_terms(i):
        if i == 0:
            for j in range(4):
                got(mbuf.at[pl.ds(pl.multiple_of(384 * other, 128), 384), pl.ds(1536 * j, 1536)], mrecv.at[j])
        lax.fori_loop(2 * i, 2 * i + 2, term_body, 0)

    def do_bpart(i):
        if i == 0:
            got(bst, wrecv)
            gather_last(0)
        gather_last(i + 1)
        shift = (0, 3 + 2 * odd, 1 + 2 * odd, 2)[i]
        pair = up(halfz + shift, NZ // 2)
        tiles, rows = [], []
        for k in range(NX):
            first = up(x + k, NX) * NZ + 2 * pair
            tiles.append(mbuf[:, pl.ds(pl.multiple_of(192 * first, 128), 384)])
            halves = []
            for block in range(2):
                found = [(e, spot) for e in range(2) for core in range(2) for spot in spots(core, block)]
                halves.append(jnp.concatenate([bbuf[first + e, a:a + n, :] for e, (a, n) in found], axis=0))
            rows.append(jnp.concatenate(halves, axis=1))
        part = jnp.dot(
            jnp.concatenate(tiles, axis=1), jnp.concatenate(rows, axis=0), preferred_element_type=F32
        )
        bacc[...] = part if i == 0 else bacc[...] + part

    def do_apass():
        for dy in (1, 3, 2):
            got(a_rows(c, dy), arecv.at[dy])
            send(a_rows(c, dy), a_rows(c, dy), asend, arecv.at[4 + dy], sib)

    def do_aturn():
        for dy in (0, 1, 3, 2):
            got(a_rows(other, dy), arecv.at[4 + dy])
        at[...] = afull[...].T

    def t_at(h, idx):
        return terms.at[idx, pl.ds(*PART[h])]

    def t_val(h, idx):
        return terms[idx, pl.ds(*PART[h]), :].astype(F32)

    order = (4, -3, 3, -2, 2, -1, 1, 0)

    def ways(off):
        odd_chunk = (z + off + NZ) % 2
        return 1 + 2 * odd_chunk, 3 - 2 * odd_chunk

    def uref(h, off, j):
        i = 24 * (h - 1) + 3 * order.index(off) + j
        return ubuf.at[i, pl.ds(0, PART[h][1])], urecv.at[i]

    def usend(src, h, off, j, k):
        dst, sem = uref(h, off, j)
        send(src, dst, rsend, sem, dev(k, 0, 0))

    def do_u(h, off):
        ahead, back = ways(off)
        usend(t_at(h, chip(2, off)), h, off, 0, ahead)
        usend(t_at(h, chip(back, off)), h, off, 1, back)

    def do_upass(h, off):
        ahead, _ = ways(off)
        ref, sem = uref(h, off, 0)
        got(ref, sem)
        ref[...] = (ref[...].astype(F32) + t_val(h, chip(ahead, off))).astype(BF16)
        usend(ref, h, off, 2, ahead)

    def usum(h, off):
        total = t_val(h, chip(0, off))
        for j in (1, 2):
            ref, sem = uref(h, off, j)
            got(ref, sem)
            total += ref[...].astype(F32)
        return total

    def zref(h, k, way, s):
        if h:
            slot = 8 * (h - 1) + 4 * way + s
            return zbuf1.at[slot, pl.ds(0, PART[h][1])], zrecv.at[32 + slot]
        slot = 8 * k + 4 * way + s
        return zbuf.at[slot], zrecv.at[slot]

    def zsend(src, h, k, way, s):
        dst, sem = zref(h, k, way, s)
        send(src, dst, rsend, sem, zup if way == 0 else zdown)

    def do_r0(k, way, s):
        lim = LEN[k][way]
        idx = chip(k, (s - lim) if way else (lim - s))
        if s == 0:
            zsend(t_at(0, idx), 0, k, way, 0)
        else:
            ref, sem = zref(0, k, way, s - 1)
            got(ref, sem)
            ref[...] = (ref[...].astype(F32) + t_val(0, idx)).astype(BF16)
            zsend(ref, 0, k, way, s)

    def do_r1(h, way, s):
        lim = LEN[4][way]
        off = (s - lim) if way else (lim - s)
        total = usum(h, off)
        if s > 0:
            ref, sem = zref(h, 4, way, s - 1)
            got(ref, sem)
            total += ref[...].astype(F32)
        mine = uref(h, off, 1)[0]
        mine[...] = total.astype(BF16)
        zsend(mine, h, 4, way, s)

    def plane():
        return [(4 * dx + dy, dx, dy) for dx in range(NX) for dy in range(NY) if dx or dy]

    def strip(a):
        return pl.ds(16 * a, 16)

    def do_orb(a):
        if a == 0:
            b_all = bacc[...]
            high = b_all.astype(BF16)
            low = (b_all - high.astype(F32)).astype(BF16)
            orb = jnp.dot(at[...], high, preferred_element_type=F32)
            orb += jnp.dot(at[...], low, preferred_element_type=F32)
            orb = orb.reshape(16, 32, BLK)
            of32[...] = orb
            obf[...] = orb.astype(BF16)
        for slot, dx, dy in plane():
            src = obf.at[up(x + dx, NX) * 4 + up(y + dy, NY), strip(a)]
            send(src, ar1.at[slot, strip(a)], osend1, orecv1.at[16 * a + slot], dev(dx, 0, dy))
        if a == 0:
            bpart[...] = high.reshape(2, NY, 96, BLK)
        if a == 1:
            for dy in range(NY):
                for oc in range(2):
                    if dy or oc:
                        core = c if oc == 0 else other
                        slot = 2 * dy + oc
                        src = bpart.at[core, up(y + dy, NY)]
                        send(src, bslots.at[slot], bsend, brecv.at[slot], dev(0, 0, dy, core))
            bslots[0] = bpart[c, y]

    def do_orb2(a):
        total = of32[4 * x + y, strip(a), :]
        for slot, _, _ in plane():
            got(ar1.at[slot, strip(a)], orecv1.at[16 * a + slot])
            total += ar1[slot, strip(a), :].astype(F32)
        mine = az.at[z, strip(a)]
        mine[...] = total.astype(BF16)
        for dz in (4, 3, 5, 2, 6, 1, 7):
            send(mine, mine, osend2, orecv2.at[8 * a + dz], dev(0, dz, 0))

    def do_orb4(a):
        for dz in range(1, NZ):
            got(az.at[up(z - dz + NZ, NZ), strip(a)], orecv2.at[8 * a + dz])
        total = az[0, strip(a), :].astype(F32)
        for i in range(1, NZ):
            total += az[i, strip(a), :].astype(F32)
        mine = rbuf.at[c, 4 * x + y, strip(a)]
        mine[...] = (total * (1.0 / math.sqrt(24576))).astype(BF16)
        for slot, dx, dy in plane():
            send(mine, mine, osend4, orecv4.at[16 * a + slot], dev(dx, 0, dy))

    def zlast(h, k):
        total = usum(h, 0) if h else t_val(0, chip(k, 0))
        for way in range(2):
            ref, sem = zref(h, k, way, LEN[k][way] - 1)
            got(ref, sem)
            total += ref[...].astype(F32)
        return total

    def do_r0x(k):
        xbuf[k] = zlast(0, k).astype(BF16)
        send(xbuf.at[k], xbuf.at[3 + k], rsend, xrecv.at[k], dev(k, 0, 0))

    pieces = {}

    def do_end0():
        total = zlast(0, 0)
        for k in (1, 3, 2):
            got(xbuf.at[3 + k], xrecv.at[k])
            total += xbuf[3 + k].astype(F32)
        pieces[0] = total
        aimg[pl.ds(pl.multiple_of(64 * odd, 8), 128), 0:128] = total[0:128, :].T
        for oc in range(2):
            total = 0.0
            for dy in range(NY):
                slot = 2 * dy + oc
                if slot:
                    got(bslots.at[slot], brecv.at[slot])
                total += bslots[slot].astype(F32)
            bwhole[c if oc == 0 else other] = total
        pltpu.make_async_copy(bwhole, b_out, outsem.at[3]).start()

    def do_end1(h):
        pieces[h] = zlast(h, 4)

    def do_orbend(a):
        for slot, dx, dy in plane():
            src = up(x - dx + NX, NX) * 4 + up(y - dy + NY, NY)
            got(rbuf.at[c, src, strip(a)], orecv4.at[16 * a + slot])
        half, there = rbuf.at[c, pl.ds(0, 16), strip(a)], r_out.at[c, pl.ds(0, 16), strip(a)]
        send(half, there, dsend, drecv.at[a], sib)
        pltpu.make_async_copy(half, there, outsem.at[a]).start()

    steps = dict(
        x0=do_x0, z0=do_z0, z1=do_z1, x1=do_x1, apass=do_apass, aturn=do_aturn, terms=do_terms, bpart=do_bpart,
        u=do_u, upass=do_upass, r0=do_r0, r1=do_r1, r0x=do_r0x, orb=do_orb, orb2=do_orb2, orb4=do_orb4,
        orbend=do_orbend, end0=do_end0, end1=do_end1,
    )
    for name, *where in ORDER:
        steps[name](*where)

    image = jnp.concatenate([pieces[h] for h in range(len(PART))], axis=0)
    for h in range(2):
        lanes = pl.ds(128 * h, 128)
        packed = image[192 * h + 128:192 * h + 192, :]
        rest = jnp.concatenate([packed, pltpu.roll(packed, 64, 1)], axis=0).T
        if h:
            aimg[pl.ds(pl.multiple_of(64 * odd, 8), 128), lanes] = image[192 * h:192 * h + 128, :].T
        aimg[pl.ds(pl.multiple_of(128 * (1 - odd), 8), 64), lanes] = rest[0:64, :]
    send(aimg.at[pl.ds(pl.multiple_of(96 * other, 8), 96)], a_out.at[c], ssend, srecv, sib)
    mine = aimg.at[pl.ds(brow, 96)]
    pltpu.make_async_copy(mine, a_out.at[c], outsem.at[2]).start()
    for a in range(2):
        got(r_out.at[other, pl.ds(0, 16), strip(a)], drecv.at[a])
        got(r_out.at[c, pl.ds(0, 16), strip(a)], outsem.at[a])
    got(bwhole, outsem.at[3])
    got(mine, outsem.at[2])

    got(bst, wsend)
    got(afull.at[pl.ds(0, 672)], asend)
    got(own_m, msend)
    got(bbuf.at[pl.ds(0, 31)], gsend)
    got(bbuf.at[pl.ds(0, 31)], rsend)
    got(bslots.at[pl.ds(1, 7)], bsend)
    got(obf.at[pl.ds(0, 15)], osend1)
    got(obf.at[pl.ds(0, 7)], osend2)
    got(obf.at[pl.ds(0, 15)], osend4)
    got(rbuf.at[c], dsend)
    got(mine, ssend)
    got(a_out.at[other], srecv)


def last_kernel(
    r_hbm, b_hbm, a_hbm, oa_hbm, ob_hbm, oo_hbm, r_ref, b_ref, a_ref, oa_ref, ob_ref, oo_ref, insem, outsem
):
    factor = 1.0 / math.sqrt(512)
    loads = [
        pltpu.make_async_copy(src, dst, insem.at[i])
        for i, (src, dst) in enumerate(((r_hbm, r_ref), (b_hbm, b_ref), (a_hbm, a_ref)))
    ]
    for load in loads:
        load.start()
    stores = []

    def store(src, dst):
        stores.append(pltpu.make_async_copy(src, dst, outsem.at[len(stores)]))
        stores[-1].start()

    loads[0].wait()
    for g in range(2):
        rows = pl.ds(BLK * g, BLK)
        for h in range(2):
            oo_ref[rows, h * BLK:(h + 1) * BLK] = r_ref[h, 8 * g:8 * g + 8].reshape(BLK, BLK).astype(F32)
        store(oo_ref.at[rows], oo_hbm.at[rows])
    loads[1].wait()
    res_a = 0.0
    for h in range(2):
        half = r_ref[h].reshape(512, BLK)
        for v in split(b_ref[h]):
            res_a += lax.dot_general(v, half, (((1,), (1,)), ((), ())), preferred_element_type=F32)
    oa_ref[...] = (res_a * factor).astype(BF16)
    store(oa_ref, oa_hbm)
    loads[2].wait()
    res_b = [0.0, 0.0]
    for h in range(2):
        for v in split(a_ref[h]):
            for j in range(2):
                rows = r_ref[j, 8 * h:8 * h + 8].reshape(BLK, BLK)
                res_b[j] += jnp.dot(v, rows, preferred_element_type=F32)
    for j in range(2):
        ob_ref[:, j * BLK:(j + 1) * BLK] = (res_b[j] * factor).astype(BF16)
    store(ob_ref, ob_hbm)
    for copy in stores:
        copy.wait()


def local(margin, margin_pattern, orbitals_a, pattern_a, orbitals_b, pattern_b):
    any_ = pl.BlockSpec(memory_space=pl.ANY)
    dma = pltpu.SemaphoreType.DMA
    later = len(LATER)

    def buf(*shape, dtype=BF16):
        return pltpu.VMEM(shape, dtype)

    middle = pl.pallas_call(
        kernel,
        out_shape=(
            jax.ShapeDtypeStruct((2, 16, 32, 256), BF16),
            jax.ShapeDtypeStruct((2, 96, 256), F32),
            jax.ShapeDtypeStruct((2, 96, 256), F32),
        ),
        in_specs=[any_] * 6,
        out_specs=(any_, any_, any_),
        scratch_shapes=[
            buf(768, 6144), buf(768, 512), buf(512, 768), buf(32, 384, 128), buf(192, 128), buf(32, 384, 128),
            buf(32, ROWS0, 128), buf(8 * later, ROWS1, 128), buf(24 * later, ROWS1, 128), buf(7, ROWS0, 128),
            buf(768, 256, dtype=F32), buf(2, 4, 96, 256), buf(8, 96, 256),
            buf(16, 32, 256, dtype=F32), buf(16, 32, 256), buf(16, 32, 256),
            buf(8, 32, 256), buf(2, 16, 32, 256), buf(192, 256, dtype=F32),
            buf(2, 96, 256, dtype=F32), buf(96, 512), buf(96, 512), pltpu.SMEM((96, 96), jnp.int32),
            pltpu.SMEM((2, 96), jnp.int32), pltpu.SMEM((2, 96), jnp.int32),
            dma, dma((5,)), dma, dma((4,)), dma, dma((8,)), dma, dma, dma, dma((CH * len(PART),)),
            dma, dma((32 + 8 * later,)), dma((24 * later,)), dma((4,)), dma, dma((8,)), dma, dma((32,)), dma, dma((16,)),
            dma, dma((32,)), dma, dma((2,)), dma, dma, dma((4,)),
        ],
        compiler_params=pltpu.CompilerParams(
            collective_id=0, has_side_effects=True, vmem_limit_bytes=60 << 20
        ),
        name="exchange",
    )(margin, margin_pattern, orbitals_a, pattern_a.T, orbitals_b, pattern_b.T)
    return pl.pallas_call(
        last_kernel,
        out_shape=(
            jax.ShapeDtypeStruct((96, 512), BF16),
            jax.ShapeDtypeStruct((96, 512), BF16),
            jax.ShapeDtypeStruct((512, 512), F32),
        ),
        in_specs=[any_, any_, any_],
        out_specs=(any_, any_, any_),
        scratch_shapes=[
            buf(2, 16, 32, 256), buf(2, 96, 256, dtype=F32), buf(2, 96, 256, dtype=F32),
            buf(96, 512), buf(96, 512), buf(512, 512, dtype=F32), dma((3,)), dma((4,)),
        ],
        compiler_params=pltpu.CompilerParams(vmem_limit_bytes=60 << 20),
        name="last",
    )(*middle)


def solution(mesh):
    in_specs = (P("row", "col"), P(), P(("row", "col"), None), P(), P(("col", "row"), None), P())
    out_specs = (P(("row", "col"), None), P(("col", "row"), None), P())
    return jax.shard_map(local, mesh=mesh, in_specs=in_specs, out_specs=out_specs, check_vma=False)
```
